32 devices in a mesh: seq: 8 (over y, x, core), tensor: 4 (over z).
Axes of the slice: x: 2, y: 2, z: 4, core: 2. Of those that a mesh axis runs over, the one named last changes fastest.
Arguments:
- queries: bfloat16 [4096, 3072], P('seq', 'tensor'), may hold values from -180 to 180, as said below
- ref_keys: bfloat16 [128, 3072], P('seq', 'tensor'), may hold values from -6 to 6
- ref_values: bfloat16 [128, 3072], P('seq', 'tensor'), may hold values from -6 to 6
- grad_out: bfloat16 [4096, 3072], P('seq', 'tensor'), may hold values from -12 to 12
- key_weight: bfloat16 [3072, 3072], P(None, 'tensor'), may hold values from -0.109375 to 0.109375
- value_weight: bfloat16 [3072, 3072], P(None, 'tensor'), may hold values from -0.109375 to 0.109375
Outputs:
- grad_queries: bfloat16 [4096, 3072], P('seq', 'tensor')
- grad_ref_rows: bfloat16 [128, 3072], P('seq', 'tensor')
The draws below stay inside these ranges and needn't reach their ends.
Inputs may be any that keep to these rules, and one draw needn't show every extreme that they name: `queries`: queries of order one, some rows larger.
All inputs are finite; a program needn't handle non-finite values.
Results may differ from the reference program's by a relative error of at most 0.015.
Values may be sent and summed in bfloat16 or wider, within the bound.
A program may use at most 128 MiB of HBM per device.

```python
import jax
import jax.numpy as jnp
from jax import lax

D = 3072
HEADS = 24
HD = 128
TOK_DEV = 512
TOKENS = 4096
REF = 128
N_SEQ = 8


def key_rows(key):
    return jnp.clip(jax.random.normal(jax.random.fold_in(key, 11), (REF, D), jnp.float32), -6.0, 6.0)


def draw_ref_keys(key, part):
    return key_rows(key).astype(jnp.bfloat16)


def draw_queries(key, part):
    base = jnp.clip(jax.random.normal(jax.random.fold_in(key, 23), (TOKENS, D), jnp.float32), -6.0, 6.0)
    return base.astype(jnp.bfloat16)


def level_of(key, extent, split, smallest, top_value):
    def one(axis_at, blocks):
        heights = jax.random.uniform(jax.random.fold_in(jax.random.fold_in(key, 6), axis_at), (blocks,), jnp.float32, smallest / len(split), top_value / len(split))
        return jnp.repeat(jnp.exp(heights), extent[axis_at] // blocks).reshape((-1,) + (1,) * (len(extent) - axis_at - 1))

    gain = one(*split[0])
    for cut in split[1:]:
        gain = gain * one(*cut)
    return gain


def scatter_about(stream_key, extent, deviation, reach, cuts=(), held_as=jnp.bfloat16):
    entries = deviation * jax.random.normal(stream_key, extent, jnp.float32)
    if cuts:
        entries = entries * level_of(stream_key, extent, cuts, -0.22, 0.18)
    return jnp.clip(entries, -reach, reach).astype(held_as)


def setup_inputs(seed: int = 0) -> dict:
    splits = jax.random.split(jax.random.key(seed), 7)
    queries = draw_queries(jax.random.fold_in(splits[6], 71), 0)
    ref_keys = draw_ref_keys(jax.random.fold_in(splits[6], 71), 0)
    ref_values = scatter_about(splits[2], (REF, D), 1.0, 6.0, ((0, 8), (1, 4)))
    grad_out = scatter_about(splits[3], (TOKENS, D), 2.0, 12.0, ((0, 8), (1, 4)))
    key_weight = scatter_about(splits[4], (D, D), D ** -0.5, 0.109375, ((1, 4),))
    value_weight = scatter_about(splits[5], (D, D), D ** -0.5, 0.109375, ((1, 4),))
    return {"queries": queries, "ref_keys": ref_keys, "ref_values": ref_values, "grad_out": grad_out, "key_weight": key_weight, "value_weight": value_weight}


def head_grads(pieces):
    query_h, key_h, value_h, grad_h = pieces
    scale = 1.0 / (HD ** 0.5)
    scores = jnp.dot(query_h, key_h.T, preferred_element_type=jnp.float32) * scale
    probs = jax.nn.softmax(scores, axis=-1)
    probs_b = probs.astype(jnp.bfloat16)
    grad_probs = jnp.dot(grad_h, value_h.T, preferred_element_type=jnp.float32)
    delta = jnp.sum(probs * grad_probs, axis=-1, keepdims=True)
    grad_scores = (probs * (grad_probs - delta)).astype(jnp.bfloat16)
    grad_query = (jnp.dot(grad_scores, key_h, preferred_element_type=jnp.float32) * scale).astype(jnp.bfloat16)
    score_blocks = grad_scores.astype(jnp.float32).reshape(N_SEQ, TOK_DEV, REF)
    prob_blocks = probs_b.astype(jnp.float32).reshape(N_SEQ, TOK_DEV, REF)
    query_blocks = query_h.astype(jnp.float32).reshape(N_SEQ, TOK_DEV, HD)
    grad_blocks = grad_h.astype(jnp.float32).reshape(N_SEQ, TOK_DEV, HD)
    key_parts = (jnp.einsum("str,std->srd", score_blocks, query_blocks) * scale).astype(jnp.bfloat16)
    value_parts = jnp.einsum("str,std->srd", prob_blocks, grad_blocks).astype(jnp.bfloat16)
    key_parts, value_parts = lax.optimization_barrier((key_parts, value_parts))
    grad_key = jnp.sum(key_parts.astype(jnp.float32), axis=0)
    grad_value = jnp.sum(value_parts.astype(jnp.float32), axis=0)
    return grad_query, grad_key, grad_value


def split_heads(matrix):
    return jnp.transpose(matrix.reshape(matrix.shape[0], HEADS, HD), (1, 0, 2))


def join_heads(stacked):
    return jnp.transpose(stacked, (1, 0, 2)).reshape(stacked.shape[1], HEADS * HD)


def reference(queries, ref_keys, ref_values, grad_out, key_weight, value_weight):
    grad_query, grad_key, grad_value = lax.map(head_grads, (split_heads(queries), split_heads(ref_keys), split_heads(ref_values), split_heads(grad_out)))
    grad_queries = join_heads(grad_query)
    key_sums = join_heads(grad_key)
    value_sums = join_heads(grad_value)
    rows = jnp.dot(key_sums, key_weight.astype(jnp.float32).T, precision=lax.Precision.HIGHEST, preferred_element_type=jnp.float32)
    rows = rows + jnp.dot(value_sums, value_weight.astype(jnp.float32).T, precision=lax.Precision.HIGHEST, preferred_element_type=jnp.float32)
    return grad_queries, rows.astype(jnp.bfloat16)
```

```python
import functools
import math

import jax
import jax.numpy as jnp
from jax import lax
from jax.experimental import pallas as pl
from jax.experimental.pallas import tpu as pltpu
from jax.sharding import PartitionSpec as P

HD = 128
SCALE = 1.0 / HD**0.5
EXP_SCALE = SCALE * math.log2(math.e)
MESH = pl.DeviceIdType.MESH
F32 = jnp.float32
BF16 = jnp.bfloat16


def each(lo, hi, body):
    if hi - lo <= 8:
        for i in range(lo, hi):
            body(i)
    else:

        def step(i, carry):
            body(i)
            return carry

        lax.fori_loop(lo, hi, step, 0)


def dot_nt(a, b):
    return lax.dot_general(a, b, (((1,), (1,)), ((), ())), preferred_element_type=F32)


def dot_tn(a, b):
    return lax.dot_general(a, b, (((0,), (0,)), ((), ())), preferred_element_type=F32)


def dot_nn(a, b):
    return jnp.dot(a, b, preferred_element_type=F32)


def attend(query, key, value, grad):
    scores = dot_nt(key, query)
    grad_probs = dot_nt(value, grad)
    top = jnp.max(scores, axis=0, keepdims=True)
    weights = jnp.exp2((scores - top) * EXP_SCALE)
    inverse = 1.0 / jnp.sum(weights, axis=0, keepdims=True)
    probs = weights * inverse
    delta = jnp.sum(probs * grad_probs, axis=0, keepdims=True)
    grad_scores = (probs * (grad_probs - delta)).astype(BF16)
    grad_query = (dot_tn(grad_scores, key) * SCALE).astype(BF16)
    grad_key = dot_nn(grad_scores, query) * SCALE
    grad_value = dot_nn(probs.astype(BF16), grad)
    return grad_query, grad_key, grad_value


def kernel(
    n,
    nt,
    groups,
    q_hbm,
    k_hbm,
    v_hbm,
    g_hbm,
    kw_hbm,
    vw_hbm,
    gq_hbm,
    rows_ref,
    q_buf,
    g_buf,
    gq_buf,
    w_buf,
    kv_buf,
    parts,
    got,
    sums,
    out_send,
    out_got,
    head_acc,
    in_sem,
    own_sem,
    w_sem,
    gq_sem,
    ag_send,
    ag_recv,
    aa_send,
    aa_recv,
    rs_send,
    rs_recv,
):
    me = lax.axis_index("seq")
    mt = lax.axis_index("tensor")
    tokens, width = q_hbm.shape
    own = k_hbm.shape[0]
    heads = width // HD
    per = heads // groups
    gw = per * HD
    out_cols = rows_ref.shape[1]
    my_rows = pl.ds(pl.multiple_of(me * own, own), own)

    own_copies = [
        pltpu.make_async_copy(k_hbm, kv_buf.at[0, my_rows], own_sem.at[0]),
        pltpu.make_async_copy(v_hbm, kv_buf.at[1, my_rows], own_sem.at[1]),
    ]
    for copy in own_copies:
        copy.start()
    in_copies = [
        pltpu.make_async_copy(q_hbm, q_buf, in_sem.at[0]),
        pltpu.make_async_copy(g_hbm, g_buf, in_sem.at[1]),
    ]
    for copy in in_copies:
        copy.start()

    barrier = pltpu.get_barrier_semaphore()

    def greet_seq(k):
        pl.semaphore_signal(
            barrier, inc=1, device_id={"seq": lax.rem(me + k, n)}, device_id_type=MESH
        )

    def greet_tensor(k):
        pl.semaphore_signal(
            barrier, inc=1, device_id={"tensor": lax.rem(mt + k, nt)}, device_id_type=MESH
        )

    each(1, nt, greet_tensor)
    each(1, n, greet_seq)
    for copy in own_copies:
        copy.wait()
    pl.semaphore_wait(barrier, n + nt - 2)

    for g in range(groups):
        cols = pl.ds(g * gw, gw)

        def send_rows(k, g=g, cols=cols):
            block = kv_buf.at[:, my_rows, cols]
            pltpu.make_async_remote_copy(
                src_ref=block,
                dst_ref=block,
                send_sem=ag_send,
                recv_sem=ag_recv.at[g],
                device_id={"seq": lax.rem(me + k, n)},
                device_id_type=MESH,
            ).start()

        each(1, n, send_rows)

    w_copies = [
        pltpu.make_async_copy(kw_hbm, w_buf.at[0], w_sem.at[0]),
        pltpu.make_async_copy(vw_hbm, w_buf.at[1], w_sem.at[1]),
    ]
    for copy in w_copies:
        copy.start()
    for copy in in_copies:
        copy.wait()

    ref_rows = n * own
    others = pl.ds(0, (n - 1) * own)
    small = ref_rows <= 256
    gq_copies = []
    for g in range(groups):
        cols = pl.ds(g * gw, gw)
        arrived = kv_buf.at[:, others, cols]
        pltpu.make_async_copy(arrived, arrived, ag_recv.at[g]).wait()

        def one_head(head):
            if isinstance(head, int):
                hc = pl.ds(head * HD, HD)
            else:
                hc = pl.ds(pl.multiple_of(head * HD, HD), HD)
            key = kv_buf[0, :, hc]
            value = kv_buf[1, :, hc]
            if small:
                grad_query, grad_key, grad_value = attend(q_buf[:, hc], key, value, g_buf[:, hc])
                gq_buf[:, hc] = grad_query
            else:
                head_acc[...] = jnp.zeros_like(head_acc)

                def chunk(c, carry):
                    tok = pl.ds(pl.multiple_of(c * HD, HD), HD)
                    gq, gk, gv = attend(q_buf[tok, hc], key, value, g_buf[tok, hc])
                    gq_buf[tok, hc] = gq
                    head_acc[0] += gk
                    head_acc[1] += gv
                    return carry

                lax.fori_loop(0, tokens // HD, chunk, 0)
                grad_key, grad_value = head_acc[0], head_acc[1]
            parts[0, :, hc] = grad_key.astype(BF16)
            parts[1, :, hc] = grad_value.astype(BF16)

        if small:
            for head in range(g * per, (g + 1) * per):
                one_head(head)
        else:
            lax.fori_loop(g * per, (g + 1) * per, lambda h, c: (one_head(h), c)[1], 0)

        def send_parts(k, g=g, cols=cols):
            to = lax.rem(me + k, n)
            pltpu.make_async_remote_copy(
                src_ref=parts.at[:, pl.ds(pl.multiple_of(to * own, own), own), cols],
                dst_ref=got.at[:, pl.ds((k - 1) * own, own), cols],
                send_sem=aa_send,
                recv_sem=aa_recv.at[g],
                device_id={"seq": to},
                device_id_type=MESH,
            ).start()

        each(1, n, send_parts)
        copy = pltpu.make_async_copy(gq_buf.at[:, cols], gq_hbm.at[:, cols], gq_sem.at[g])
        copy.start()
        gq_copies.append(copy)

    for copy in w_copies:
        copy.wait()
    rs_copies = []
    for g in range(groups):
        cols = pl.ds(g * gw, gw)
        arrived = got.at[:, :, cols]
        pltpu.make_async_copy(arrived, arrived, aa_recv.at[g]).wait()
        sides = []
        for side in range(2):
            total = parts[side, my_rows, cols].astype(F32)
            if n <= 8:
                for k in range(n - 1):
                    total += got[side, k * own : (k + 1) * own, cols].astype(F32)
            else:
                total = lax.fori_loop(
                    0,
                    n - 1,
                    lambda k, acc: acc
                    + got[side, pl.ds(pl.multiple_of(k * own, own), own), cols].astype(F32),
                    total,
                )
            high = total.astype(BF16)
            low = (total - high.astype(F32)).astype(BF16)
            sides.append(jnp.concatenate([high, low], axis=0))
        for j in range(1, nt + 1):
            to = lax.rem(mt + j, nt)
            wr = pl.ds(pl.multiple_of(to * out_cols, out_cols), out_cols)
            both = dot_nt(sides[0], w_buf[0, wr, cols]) + dot_nt(sides[1], w_buf[1, wr, cols])
            new = both[:own] + both[own:]
            if g:
                new = new + sums[j - 1]
            if g < groups - 1 or j == nt:
                sums[j - 1] = new
            else:
                out_send[j - 1] = new.astype(BF16)
                copy = pltpu.make_async_remote_copy(
                    src_ref=out_send.at[j - 1],
                    dst_ref=out_got.at[j - 1],
                    send_sem=rs_send.at[j - 1],
                    recv_sem=rs_recv.at[j - 1],
                    device_id={"tensor": to},
                    device_id_type=MESH,
                )
                copy.start()
                rs_copies.append(copy)

    sent = kv_buf.at[:, others]
    pltpu.make_async_copy(sent, sent, ag_send).wait()
    pltpu.make_async_copy(got, got, aa_send).wait()
    for copy in gq_copies:
        copy.wait()
    total = sums[nt - 1]
    for j, copy in enumerate(rs_copies):
        copy.wait_recv()
        total += out_got[j].astype(F32)
    rows_ref[...] = total.astype(BF16)
    for copy in rs_copies:
        copy.wait_send()


def solution(mesh):
    n, nt = mesh.shape["seq"], mesh.shape["tensor"]

    def shards(queries, ref_keys, ref_values, grad_out, key_weight, value_weight):
        tokens, width = queries.shape
        own = ref_keys.shape[0]
        features = key_weight.shape[0]
        heads = width // HD
        groups = 3 if heads % 3 == 0 else 1
        out_cols = features // nt
        any_spec = pl.BlockSpec(memory_space=pl.ANY)
        dma = pltpu.SemaphoreType.DMA
        return pl.pallas_call(
            functools.partial(kernel, n, nt, groups),
            out_shape=(
                jax.ShapeDtypeStruct((tokens, width), BF16),
                jax.ShapeDtypeStruct((own, out_cols), BF16),
            ),
            in_specs=[any_spec] * 6,
            out_specs=(any_spec, pl.BlockSpec(memory_space=pltpu.VMEM)),
            scratch_shapes=[
                pltpu.VMEM((tokens, width), BF16),
                pltpu.VMEM((tokens, width), BF16),
                pltpu.VMEM((tokens, width), BF16),
                pltpu.VMEM((2, features, width), BF16),
                pltpu.VMEM((2, n * own, width), BF16),
                pltpu.VMEM((2, n * own, width), BF16),
                pltpu.VMEM((2, (n - 1) * own, width), BF16),
                pltpu.VMEM((nt, own, out_cols), F32),
                pltpu.VMEM((nt - 1, own, out_cols), BF16),
                pltpu.VMEM((nt - 1, own, out_cols), BF16),
                pltpu.VMEM((2, n * own, HD), F32),
                dma((2,)),
                dma((2,)),
                dma((2,)),
                dma((groups,)),
                dma,
                dma((groups,)),
                dma,
                dma((groups,)),
                dma((nt - 1,)),
                dma((nt - 1,)),
            ],
            compiler_params=pltpu.CompilerParams(
                collective_id=0,
                has_side_effects=True,
                vmem_limit_bytes=48 * 1024 * 1024,
            ),
            cost_estimate=pl.CostEstimate(
                flops=1_000_000_000, bytes_accessed=12_000_000, transcendentals=400_000
            ),
        )(queries, ref_keys, ref_values, grad_out, key_weight, value_weight)

    placed = (
        P("seq", "tensor"),
        P("seq", "tensor"),
        P("seq", "tensor"),
        P("seq", "tensor"),
        P(None, "tensor"),
        P(None, "tensor"),
    )
    return jax.shard_map(
        shards,
        mesh=mesh,
        in_specs=placed,
        out_specs=(P("seq", "tensor"), P("seq", "tensor")),
        check_vma=False,
    )
```

```python
import functools
import math

import jax
import jax.numpy as jnp
from jax import lax
from jax.experimental import pallas as pl
from jax.experimental.pallas import tpu as pltpu
from jax.sharding import PartitionSpec as P

HD = 128
CHUNK = 256
VMEM_LIMIT = 60 * 1024 * 1024
SCALE = 1.0 / HD**0.5
EXP_SCALE = SCALE * math.log2(math.e)
MESH = pl.DeviceIdType.MESH
F32 = jnp.float32
BF16 = jnp.bfloat16


def each(lo, hi, body):
    if hi - lo <= 8:
        for i in range(lo, hi):
            body(i)
    else:

        def step(i, carry):
            body(i)
            return carry

        lax.fori_loop(lo, hi, step, 0)


def dot_nt(a, b):
    return lax.dot_general(a, b, (((1,), (1,)), ((), ())), preferred_element_type=F32)


def dot_tn(a, b):
    return lax.dot_general(a, b, (((0,), (0,)), ((), ())), preferred_element_type=F32)


def dot_nn(a, b):
    return jnp.dot(a, b, preferred_element_type=F32)


def attend(query, key, value, grad):
    scores = dot_nt(key, query)
    grad_probs = dot_nt(value, grad)
    top = jnp.max(scores, axis=0, keepdims=True)
    weights = jnp.exp2((scores - top) * EXP_SCALE)
    inverse = 1.0 / jnp.sum(weights, axis=0, keepdims=True)
    probs = weights * inverse
    delta = jnp.sum(probs * grad_probs, axis=0, keepdims=True)
    grad_scores = (probs * (grad_probs - delta)).astype(BF16)
    grad_key = dot_nn(grad_scores, query)
    grad_value = dot_nn(probs.astype(BF16), grad)
    return grad_scores, grad_key, grad_value


def kernel(
    n,
    nt,
    groups,
    q_hbm,
    k_hbm,
    v_hbm,
    g_hbm,
    kw_hbm,
    vw_hbm,
    gq_hbm,
    rows_ref,
    q_buf,
    g_buf,
    gq_buf,
    ds_buf,
    w_buf,
    kv_buf,
    parts,
    got,
    sums,
    out_send,
    out_got,
    head_acc,
    in_sem,
    own_sem,
    w_sem,
    gq_sem,
    ag_send,
    ag_recv,
    aa_send,
    aa_recv,
    rs_send,
    rs_recv,
):
    me = lax.axis_index("seq")
    mt = lax.axis_index("tensor")
    tokens, width = q_hbm.shape
    own = k_hbm.shape[0]
    heads = width // HD
    per = heads // groups
    gw = per * HD
    out_cols = rows_ref.shape[1]
    my_rows = pl.ds(pl.multiple_of(me * own, own), own)

    own_copies = [
        pltpu.make_async_copy(k_hbm, kv_buf.at[0, my_rows], own_sem.at[0]),
        pltpu.make_async_copy(v_hbm, kv_buf.at[1, my_rows], own_sem.at[1]),
    ]
    for copy in own_copies:
        copy.start()
    in_copies = [
        pltpu.make_async_copy(q_hbm, q_buf, in_sem.at[0]),
        pltpu.make_async_copy(g_hbm, g_buf, in_sem.at[1]),
    ]
    for copy in in_copies:
        copy.start()

    barrier = pltpu.get_barrier_semaphore()

    def greet_seq(k):
        pl.semaphore_signal(
            barrier, inc=1, device_id={"seq": lax.rem(me + k, n)}, device_id_type=MESH
        )

    def greet_tensor(k):
        pl.semaphore_signal(
            barrier, inc=1, device_id={"tensor": lax.rem(mt + k, nt)}, device_id_type=MESH
        )

    each(1, nt, greet_tensor)
    each(1, n, greet_seq)
    for copy in own_copies:
        copy.wait()
    pl.semaphore_wait(barrier, n + nt - 2)

    for g in range(groups):
        cols = pl.ds(g * gw, gw)

        def send_rows(k, g=g, cols=cols):
            block = kv_buf.at[:, my_rows, cols]
            pltpu.make_async_remote_copy(
                src_ref=block,
                dst_ref=block,
                send_sem=ag_send,
                recv_sem=ag_recv.at[g],
                device_id={"seq": lax.rem(me + k, n)},
                device_id_type=MESH,
            ).start()

        each(1, n, send_rows)

    w_copies = [
        pltpu.make_async_copy(kw_hbm, w_buf.at[0], w_sem.at[0]),
        pltpu.make_async_copy(vw_hbm, w_buf.at[1], w_sem.at[1]),
    ]
    for copy in w_copies:
        copy.start()
    for copy in in_copies:
        copy.wait()

    ref_rows = n * own
    others = pl.ds(0, (n - 1) * own)
    small = ref_rows <= 256
    for g in range(groups):
        cols = pl.ds(g * gw, gw)
        arrived = kv_buf.at[:, others, cols]
        pltpu.make_async_copy(arrived, arrived, ag_recv.at[g]).wait()

        def one_head(head):
            if isinstance(head, int):
                hc = pl.ds(head * HD, HD)
            else:
                hc = pl.ds(pl.multiple_of(head * HD, HD), HD)
            key = kv_buf[0, :, hc]
            value = kv_buf[1, :, hc]
            if small:
                grad_key = grad_value = None
                for lo in range(0, tokens, CHUNK):
                    tok = slice(lo, min(lo + CHUNK, tokens))
                    ds, gk, gv = attend(q_buf[tok, hc], key, value, g_buf[tok, hc])
                    ds_buf[head, :, tok] = ds
                    grad_key = gk if grad_key is None else grad_key + gk
                    grad_value = gv if grad_value is None else grad_value + gv
            else:
                head_acc[...] = jnp.zeros_like(head_acc)

                def chunk(c, carry):
                    tok = pl.ds(pl.multiple_of(c * HD, HD), HD)
                    ds, gk, gv = attend(q_buf[tok, hc], key, value, g_buf[tok, hc])
                    ds_buf[head, :, tok] = ds
                    head_acc[0] += gk
                    head_acc[1] += gv
                    return carry

                lax.fori_loop(0, tokens // HD, chunk, 0)
                grad_key, grad_value = head_acc[0], head_acc[1]
            parts[0, :, hc] = (grad_key * SCALE).astype(BF16)
            parts[1, :, hc] = grad_value.astype(BF16)

        if small:
            for head in range(g * per, (g + 1) * per):
                one_head(head)
        else:
            lax.fori_loop(g * per, (g + 1) * per, lambda h, c: (one_head(h), c)[1], 0)

        def send_parts(k, g=g, cols=cols):
            to = lax.rem(me + k, n)
            pltpu.make_async_remote_copy(
                src_ref=parts.at[:, pl.ds(pl.multiple_of(to * own, own), own), cols],
                dst_ref=got.at[:, pl.ds((k - 1) * own, own), cols],
                send_sem=aa_send,
                recv_sem=aa_recv.at[g],
                device_id={"seq": to},
                device_id_type=MESH,
            ).start()

        each(1, n, send_parts)

    gq_copies = []

    def query_grads(g):
        def one_head(head):
            if isinstance(head, int):
                hc = pl.ds(head * HD, HD)
            else:
                hc = pl.ds(pl.multiple_of(head * HD, HD), HD)
            gq_buf[:, hc] = (dot_tn(ds_buf[head], kv_buf[0, :, hc]) * SCALE).astype(BF16)

        if small:
            for head in range(g * per, (g + 1) * per):
                one_head(head)
        else:
            lax.fori_loop(g * per, (g + 1) * per, lambda h, c: (one_head(h), c)[1], 0)
        cols = pl.ds(g * gw, gw)
        copy = pltpu.make_async_copy(gq_buf.at[:, cols], gq_hbm.at[:, cols], gq_sem.at[g])
        copy.start()
        gq_copies.append(copy)

    for copy in w_copies:
        copy.wait()
    rs_copies = []
    for g in range(groups):
        if g < groups - 1:
            query_grads(g)
        cols = pl.ds(g * gw, gw)
        arrived = got.at[:, :, cols]
        pltpu.make_async_copy(arrived, arrived, aa_recv.at[g]).wait()
        sides = []
        for side in range(2):
            total = parts[side, my_rows, cols].astype(F32)
            if n <= 8:
                for k in range(n - 1):
                    total += got[side, k * own : (k + 1) * own, cols].astype(F32)
            else:
                total = lax.fori_loop(
                    0,
                    n - 1,
                    lambda k, acc: acc
                    + got[side, pl.ds(pl.multiple_of(k * own, own), own), cols].astype(F32),
                    total,
                )
            high = total.astype(BF16)
            low = (total - high.astype(F32)).astype(BF16)
            sides.append(jnp.concatenate([high, low], axis=0))
        for j in range(1, nt + 1):
            to = lax.rem(mt + j, nt)
            wr = pl.ds(pl.multiple_of(to * out_cols, out_cols), out_cols)
            both = dot_nt(sides[0], w_buf[0, wr, cols]) + dot_nt(sides[1], w_buf[1, wr, cols])
            new = both[:own] + both[own:]
            if g:
                new = new + sums[j - 1]
            if g < groups - 1 or j == nt:
                sums[j - 1] = new
            else:
                out_send[j - 1] = new.astype(BF16)
                copy = pltpu.make_async_remote_copy(
                    src_ref=out_send.at[j - 1],
                    dst_ref=out_got.at[j - 1],
                    send_sem=rs_send.at[j - 1],
                    recv_sem=rs_recv.at[j - 1],
                    device_id={"tensor": to},
                    device_id_type=MESH,
                )
                copy.start()
                rs_copies.append(copy)

    query_grads(groups - 1)
    sent = kv_buf.at[:, others]
    pltpu.make_async_copy(sent, sent, ag_send).wait()
    pltpu.make_async_copy(got, got, aa_send).wait()
    for copy in gq_copies[:-1]:
        copy.wait()
    total = sums[nt - 1]
    for j, copy in enumerate(rs_copies):
        copy.wait_recv()
        total += out_got[j].astype(F32)
    rows_ref[...] = total.astype(BF16)
    for copy in rs_copies:
        copy.wait_send()
    gq_copies[-1].wait()


def deliver(gq_ref, rows_ref, gq_out, rows_out, sem):
    copies = [
        pltpu.make_async_copy(gq_ref, gq_out, sem.at[0]),
        pltpu.make_async_copy(rows_ref, rows_out, sem.at[1]),
    ]
    for copy in copies:
        copy.start()
    for copy in copies:
        copy.wait()


def solution(mesh):
    n, nt = mesh.shape["seq"], mesh.shape["tensor"]

    def shards(queries, ref_keys, ref_values, grad_out, key_weight, value_weight):
        tokens, width = queries.shape
        own = ref_keys.shape[0]
        features = key_weight.shape[0]
        heads = width // HD
        groups = 3 if heads % 3 == 0 else 1
        out_cols = features // nt
        hbm_spec = pl.BlockSpec(memory_space=pltpu.HBM)
        vmem_spec = pl.BlockSpec(memory_space=pltpu.VMEM)
        dma = pltpu.SemaphoreType.DMA
        held = pl.pallas_call(
            functools.partial(kernel, n, nt, groups),
            out_shape=(
                jax.ShapeDtypeStruct((tokens, width), BF16),
                jax.ShapeDtypeStruct((own, out_cols), BF16),
            ),
            in_specs=[hbm_spec] * 6,
            out_specs=(hbm_spec, vmem_spec),
            scratch_shapes=[
                pltpu.VMEM((tokens, width), BF16),
                pltpu.VMEM((tokens, width), BF16),
                pltpu.VMEM((tokens, width), BF16),
                pltpu.VMEM((heads, n * own, tokens), BF16),
                pltpu.VMEM((2, features, width), BF16),
                pltpu.VMEM((2, n * own, width), BF16),
                pltpu.VMEM((2, n * own, width), BF16),
                pltpu.VMEM((2, (n - 1) * own, width), BF16),
                pltpu.VMEM((nt, own, out_cols), F32),
                pltpu.VMEM((nt - 1, own, out_cols), BF16),
                pltpu.VMEM((nt - 1, own, out_cols), BF16),
                pltpu.VMEM((2, n * own, HD), F32),
                dma((2,)),
                dma((2,)),
                dma((2,)),
                dma((groups,)),
                dma,
                dma((groups,)),
                dma,
                dma((groups,)),
                dma((nt - 1,)),
                dma((nt - 1,)),
            ],
            compiler_params=pltpu.CompilerParams(
                collective_id=0,
                has_side_effects=True,
                vmem_limit_bytes=VMEM_LIMIT,
            ),
            cost_estimate=pl.CostEstimate(
                flops=1_000_000_000, bytes_accessed=12_000_000, transcendentals=400_000
            ),
        )(queries, ref_keys, ref_values, grad_out, key_weight, value_weight)
        return pl.pallas_call(
            deliver,
            out_shape=(
                jax.ShapeDtypeStruct((tokens, width), BF16),
                jax.ShapeDtypeStruct((own, out_cols), BF16),
            ),
            in_specs=[hbm_spec] * 2,
            out_specs=(hbm_spec, hbm_spec),
            scratch_shapes=[dma((2,))],
            compiler_params=pltpu.CompilerParams(vmem_limit_bytes=VMEM_LIMIT),
        )(*held)

    placed = (
        P("seq", "tensor"),
        P("seq", "tensor"),
        P("seq", "tensor"),
        P("seq", "tensor"),
        P(None, "tensor"),
        P(None, "tensor"),
    )
    return jax.shard_map(
        shards,
        mesh=mesh,
        in_specs=placed,
        out_specs=(P("seq", "tensor"), P("seq", "tensor")),
        check_vma=False,
    )
```

```python
import functools
import math

import jax
import jax.numpy as jnp
from jax import lax
from jax.experimental import pallas as pl
from jax.experimental.pallas import tpu as pltpu
from jax.sharding import PartitionSpec as P

HD = 128
CHUNK = 256
SPLIT = 4
VMEM_LIMIT = 48 * 1024 * 1024
SCALE = 1.0 / HD**0.5
EXP_SCALE = SCALE * math.log2(math.e)
MESH = pl.DeviceIdType.MESH
F32 = jnp.float32
BF16 = jnp.bfloat16


def each(lo, hi, body):
    if hi - lo <= 8:
        for i in range(lo, hi):
            body(i)
    else:

        def step(i, carry):
            body(i)
            return carry

        lax.fori_loop(lo, hi, step, 0)


def dot_nt(a, b):
    return lax.dot_general(a, b, (((1,), (1,)), ((), ())), preferred_element_type=F32)


def dot_tn(a, b):
    return lax.dot_general(a, b, (((0,), (0,)), ((), ())), preferred_element_type=F32)


def dot_nn(a, b):
    return jnp.dot(a, b, preferred_element_type=F32)


def attend(query, key, value, grad):
    scores = dot_nt(key, query)
    grad_probs = dot_nt(value, grad)
    top = jnp.max(scores, axis=0, keepdims=True)
    weights = jnp.exp2((scores - top) * EXP_SCALE)
    inverse = 1.0 / jnp.sum(weights, axis=0, keepdims=True)
    probs = weights * inverse
    delta = jnp.sum(probs * grad_probs, axis=0, keepdims=True)
    grad_scores = (probs * (grad_probs - delta)).astype(BF16)
    grad_key = dot_nn(grad_scores, query)
    grad_value = dot_nn(probs.astype(BF16), grad)
    return grad_scores, grad_key, grad_value


def kernel(
    n,
    nt,
    groups,
    q_hbm,
    k_hbm,
    v_hbm,
    g_hbm,
    kw_hbm,
    vw_hbm,
    gq_buf,
    rows_ref,
    q_buf,
    g_buf,
    ds_buf,
    w_buf,
    kv_buf,
    parts,
    got,
    sums,
    out_send,
    out_got,
    head_acc,
    in_sem,
    own_sem,
    w_sem,
    ag_send,
    ag_recv,
    aa_send,
    aa_recv,
    rs_send,
    rs_recv,
):
    me = lax.axis_index("seq")
    mt = lax.axis_index("tensor")
    tokens, width = q_hbm.shape
    own = k_hbm.shape[0]
    heads = width // HD
    per = heads // groups
    gw = per * HD
    out_cols = rows_ref.shape[1]
    my_rows = pl.ds(pl.multiple_of(me * own, own), own)

    own_copies = [
        pltpu.make_async_copy(k_hbm, kv_buf.at[0, my_rows], own_sem.at[0]),
        pltpu.make_async_copy(v_hbm, kv_buf.at[1, my_rows], own_sem.at[1]),
    ]
    for copy in own_copies:
        copy.start()
    in_copies = [
        pltpu.make_async_copy(q_hbm, q_buf, in_sem.at[0]),
        pltpu.make_async_copy(g_hbm, g_buf, in_sem.at[1]),
    ]
    for copy in in_copies:
        copy.start()

    barrier = pltpu.get_barrier_semaphore()

    def greet_seq(k):
        pl.semaphore_signal(
            barrier, inc=1, device_id={"seq": lax.rem(me + k, n)}, device_id_type=MESH
        )

    def greet_tensor(k):
        pl.semaphore_signal(
            barrier, inc=1, device_id={"tensor": lax.rem(mt + k, nt)}, device_id_type=MESH
        )

    each(1, nt, greet_tensor)
    each(1, n, greet_seq)
    for copy in own_copies:
        copy.wait()
    pl.semaphore_wait(barrier, n + nt - 2)

    for g in range(groups):
        cols = pl.ds(g * gw, gw)

        def send_rows(k, g=g, cols=cols):
            block = kv_buf.at[:, my_rows, cols]
            pltpu.make_async_remote_copy(
                src_ref=block,
                dst_ref=block,
                send_sem=ag_send,
                recv_sem=ag_recv.at[g],
                device_id={"seq": lax.rem(me + k, n)},
                device_id_type=MESH,
            ).start()

        each(1, n, send_rows)

    w_copies = [
        pltpu.make_async_copy(kw_hbm, w_buf.at[0], w_sem.at[0]),
        pltpu.make_async_copy(vw_hbm, w_buf.at[1], w_sem.at[1]),
    ]
    for copy in w_copies:
        copy.start()
    for copy in in_copies:
        copy.wait()

    ref_rows = n * own
    others = pl.ds(0, (n - 1) * own)
    small = ref_rows <= 256
    for g in range(groups):
        cols = pl.ds(g * gw, gw)
        arrived = kv_buf.at[:, others, cols]
        pltpu.make_async_copy(arrived, arrived, ag_recv.at[g]).wait()

        def one_head(head):
            if isinstance(head, int):
                hc = pl.ds(head * HD, HD)
            else:
                hc = pl.ds(pl.multiple_of(head * HD, HD), HD)
            key = kv_buf[0, :, hc]
            value = kv_buf[1, :, hc]
            if small:
                grad_key = grad_value = None
                for lo in range(0, tokens, CHUNK):
                    tok = slice(lo, min(lo + CHUNK, tokens))
                    ds, gk, gv = attend(q_buf[tok, hc], key, value, g_buf[tok, hc])
                    ds_buf[head, :, tok] = ds
                    grad_key = gk if grad_key is None else grad_key + gk
                    grad_value = gv if grad_value is None else grad_value + gv
            else:
                head_acc[...] = jnp.zeros_like(head_acc)

                def chunk(c, carry):
                    tok = pl.ds(pl.multiple_of(c * HD, HD), HD)
                    ds, gk, gv = attend(q_buf[tok, hc], key, value, g_buf[tok, hc])
                    ds_buf[head, :, tok] = ds
                    head_acc[0] += gk
                    head_acc[1] += gv
                    return carry

                lax.fori_loop(0, tokens // HD, chunk, 0)
                grad_key, grad_value = head_acc[0], head_acc[1]
            parts[0, :, hc] = (grad_key * SCALE).astype(BF16)
            parts[1, :, hc] = grad_value.astype(BF16)

        if small:
            for head in range(g * per, (g + 1) * per):
                one_head(head)
        else:
            lax.fori_loop(g * per, (g + 1) * per, lambda h, c: (one_head(h), c)[1], 0)

        def send_parts(k, g=g, cols=cols):
            to = lax.rem(me + k, n)
            pltpu.make_async_remote_copy(
                src_ref=parts.at[:, pl.ds(pl.multiple_of(to * own, own), own), cols],
                dst_ref=got.at[:, pl.ds((k - 1) * own, own), cols],
                send_sem=aa_send,
                recv_sem=aa_recv.at[g],
                device_id={"seq": to},
                device_id_type=MESH,
            ).start()

        each(1, n, send_parts)

    def query_grads(g):
        def one_head(head):
            if isinstance(head, int):
                hc = pl.ds(head * HD, HD)
            else:
                hc = pl.ds(pl.multiple_of(head * HD, HD), HD)
            gq_buf[:, hc] = (dot_tn(ds_buf[head], kv_buf[0, :, hc]) * SCALE).astype(BF16)

        if small:
            for head in range(g * per, (g + 1) * per):
                one_head(head)
        else:
            lax.fori_loop(g * per, (g + 1) * per, lambda h, c: (one_head(h), c)[1], 0)

    for copy in w_copies:
        copy.wait()
    rs_copies = []
    for g in range(groups):
        if g < groups - 1:
            query_grads(g)
        cols = pl.ds(g * gw, gw)
        arrived = got.at[:, :, cols]
        pltpu.make_async_copy(arrived, arrived, aa_recv.at[g]).wait()
        sides = []
        for side in range(2):
            total = parts[side, my_rows, cols].astype(F32)
            if n <= 8:
                for k in range(n - 1):
                    total += got[side, k * own : (k + 1) * own, cols].astype(F32)
            else:
                total = lax.fori_loop(
                    0,
                    n - 1,
                    lambda k, acc: acc
                    + got[side, pl.ds(pl.multiple_of(k * own, own), own), cols].astype(F32),
                    total,
                )
            high = total.astype(BF16)
            low = (total - high.astype(F32)).astype(BF16)
            sides.append(jnp.concatenate([high, low], axis=0))
        for j in range(1, nt + 1):
            to = lax.rem(mt + j, nt)
            wr = pl.ds(pl.multiple_of(to * out_cols, out_cols), out_cols)
            both = dot_nt(sides[0], w_buf[0, wr, cols]) + dot_nt(sides[1], w_buf[1, wr, cols])
            new = both[:own] + both[own:]
            if g:
                new = new + sums[j - 1]
            if g < groups - 1 or j == nt:
                sums[j - 1] = new
            else:
                out_send[j - 1] = new.astype(BF16)
                copy = pltpu.make_async_remote_copy(
                    src_ref=out_send.at[j - 1],
                    dst_ref=out_got.at[j - 1],
                    send_sem=rs_send.at[j - 1],
                    recv_sem=rs_recv.at[j - 1],
                    device_id={"tensor": to},
                    device_id_type=MESH,
                )
                copy.start()
                rs_copies.append(copy)

    query_grads(groups - 1)
    sent = kv_buf.at[:, others]
    pltpu.make_async_copy(sent, sent, ag_send).wait()
    pltpu.make_async_copy(got, got, aa_send).wait()
    total = sums[nt - 1]
    for j, copy in enumerate(rs_copies):
        copy.wait_recv()
        total += out_got[j].astype(F32)
    rows_ref[...] = total.astype(BF16)
    for copy in rs_copies:
        copy.wait_send()


def deliver(gq_ref, rows_ref, gq_out, rows_out, sem):
    part = gq_ref.shape[0] // SPLIT
    copies = [pltpu.make_async_copy(rows_ref, rows_out, sem.at[SPLIT])]
    for i in range(SPLIT):
        rows = pl.ds(i * part, part)
        copies.append(pltpu.make_async_copy(gq_ref.at[rows], gq_out.at[rows], sem.at[i]))
    for copy in copies:
        copy.start()
    for copy in copies:
        copy.wait()


def solution(mesh):
    n, nt = mesh.shape["seq"], mesh.shape["tensor"]

    def shards(queries, ref_keys, ref_values, grad_out, key_weight, value_weight):
        tokens, width = queries.shape
        own = ref_keys.shape[0]
        features = key_weight.shape[0]
        heads = width // HD
        groups = 3 if heads % 3 == 0 else 1
        out_cols = features // nt
        hbm_spec = pl.BlockSpec(memory_space=pltpu.HBM)
        vmem_spec = pl.BlockSpec(memory_space=pltpu.VMEM)
        dma = pltpu.SemaphoreType.DMA
        held = pl.pallas_call(
            functools.partial(kernel, n, nt, groups),
            out_shape=(
                pltpu.VMEM((tokens, width), BF16),
                pltpu.VMEM((own, out_cols), BF16),
            ),
            in_specs=[hbm_spec] * 6,
            out_specs=(vmem_spec, vmem_spec),
            scratch_shapes=[
                pltpu.VMEM((tokens, width), BF16),
                pltpu.VMEM((tokens, width), BF16),
                pltpu.VMEM((heads, n * own, tokens), BF16),
                pltpu.VMEM((2, features, width), BF16),
                pltpu.VMEM((2, n * own, width), BF16),
                pltpu.VMEM((2, n * own, width), BF16),
                pltpu.VMEM((2, (n - 1) * own, width), BF16),
                pltpu.VMEM((nt, own, out_cols), F32),
                pltpu.VMEM((nt - 1, own, out_cols), BF16),
                pltpu.VMEM((nt - 1, own, out_cols), BF16),
                pltpu.VMEM((2, n * own, HD), F32),
                dma((2,)),
                dma((2,)),
                dma((2,)),
                dma,
                dma((groups,)),
                dma,
                dma((groups,)),
                dma((nt - 1,)),
                dma((nt - 1,)),
            ],
            compiler_params=pltpu.CompilerParams(
                collective_id=0,
                has_side_effects=True,
                vmem_limit_bytes=VMEM_LIMIT,
            ),
            cost_estimate=pl.CostEstimate(
                flops=1_000_000_000, bytes_accessed=12_000_000, transcendentals=400_000
            ),
        )(
            *(
                pltpu.with_memory_space_constraint(x, pltpu.HBM)
                for x in (queries, ref_keys, ref_values, grad_out, key_weight, value_weight)
            )
        )
        return pl.pallas_call(
            deliver,
            out_shape=(
                jax.ShapeDtypeStruct((tokens, width), BF16),
                jax.ShapeDtypeStruct((own, out_cols), BF16),
            ),
            in_specs=[vmem_spec] * 2,
            out_specs=(hbm_spec, hbm_spec),
            scratch_shapes=[dma((SPLIT + 1,))],
        )(*held)

    placed = (
        P("seq", "tensor"),
        P("seq", "tensor"),
        P("seq", "tensor"),
        P("seq", "tensor"),
        P(None, "tensor"),
        P(None, "tensor"),
    )
    return jax.shard_map(
        shards,
        mesh=mesh,
        in_specs=placed,
        out_specs=(P("seq", "tensor"), P("seq", "tensor")),
        check_vma=False,
    )
```

```python
import functools
import math

import jax
import jax.numpy as jnp
from jax import lax
from jax.experimental import pallas as pl
from jax.experimental.pallas import tpu as pltpu
from jax.sharding import PartitionSpec as P

HD = 128
CHUNK = 256
SPLIT = 4
VMEM_LIMIT = 48 * 1024 * 1024
SCALE = 1.0 / HD**0.5
EXP_SCALE = SCALE * math.log2(math.e)
MESH = pl.DeviceIdType.MESH
F32 = jnp.float32
BF16 = jnp.bfloat16


def each(lo, hi, body):
    if hi - lo <= 8:
        for i in range(lo, hi):
            body(i)
    else:

        def step(i, carry):
            body(i)
            return carry

        lax.fori_loop(lo, hi, step, 0)


def dot_nt(a, b):
    return lax.dot_general(a, b, (((1,), (1,)), ((), ())), preferred_element_type=F32)


def dot_tn(a, b):
    return lax.dot_general(a, b, (((0,), (0,)), ((), ())), preferred_element_type=F32)


def dot_nn(a, b):
    return jnp.dot(a, b, preferred_element_type=F32)


def attend(query, key, value, grad):
    scores = dot_nt(key, query)
    grad_probs = dot_nt(value, grad)
    top = jnp.max(scores, axis=0, keepdims=True)
    weights = jnp.exp2((scores - top) * EXP_SCALE)
    inverse = 1.0 / jnp.sum(weights, axis=0, keepdims=True)
    probs = weights * inverse
    delta = jnp.sum(probs * grad_probs, axis=0, keepdims=True)
    grad_scores = (probs * (grad_probs - delta)).astype(BF16)
    grad_key = dot_nn(grad_scores, query)
    grad_value = dot_nn(probs.astype(BF16), grad)
    return grad_scores, grad_key, grad_value


def kernel(
    n,
    nt,
    groups,
    cuts,
    q_hbm,
    k_hbm,
    v_hbm,
    g_hbm,
    kw_hbm,
    vw_hbm,
    gq_buf,
    rows_ref,
    q_buf,
    g_buf,
    ds_buf,
    w_buf,
    kv_buf,
    parts,
    got,
    sums,
    out_send,
    out_got,
    head_acc,
    in_sem,
    own_sem,
    w_sem,
    ag_send,
    ag_recv,
    aa_send,
    aa_recv,
    rs_send,
    rs_recv,
):
    me = lax.axis_index("seq")
    mt = lax.axis_index("tensor")
    tokens, width = q_hbm.shape
    own = k_hbm.shape[0]
    heads = width // HD
    per = heads // groups
    gw = per * HD
    out_cols = rows_ref.shape[1]
    my_rows = pl.ds(pl.multiple_of(me * own, own), own)

    barrier = pltpu.get_barrier_semaphore()

    def greet_seq(k):
        pl.semaphore_signal(
            barrier, inc=1, device_id={"seq": lax.rem(me + k, n)}, device_id_type=MESH
        )

    def greet_tensor(k):
        pl.semaphore_signal(
            barrier, inc=1, device_id={"tensor": lax.rem(mt + k, nt)}, device_id_type=MESH
        )

    each(1, n, greet_seq)
    each(1, nt, greet_tensor)
    own_copies = [
        pltpu.make_async_copy(k_hbm, kv_buf.at[0, my_rows], own_sem.at[0]),
        pltpu.make_async_copy(v_hbm, kv_buf.at[1, my_rows], own_sem.at[1]),
    ]
    for copy in own_copies:
        copy.start()
    in_copies = [
        pltpu.make_async_copy(q_hbm, q_buf, in_sem.at[0]),
        pltpu.make_async_copy(g_hbm, g_buf, in_sem.at[1]),
    ]
    for copy in in_copies:
        copy.start()

    for copy in own_copies:
        copy.wait()
    pl.semaphore_wait(barrier, n + nt - 2)

    for c, (first, count) in enumerate(cuts):
        cols = pl.ds(first * HD, count * HD)

        def send_rows(k, c=c, cols=cols):
            block = kv_buf.at[:, my_rows, cols]
            pltpu.make_async_remote_copy(
                src_ref=block,
                dst_ref=block,
                send_sem=ag_send,
                recv_sem=ag_recv.at[c],
                device_id={"seq": lax.rem(me + k, n)},
                device_id_type=MESH,
            ).start()

        each(1, n, send_rows)

    w_copies = [
        pltpu.make_async_copy(kw_hbm, w_buf.at[0], w_sem.at[0]),
        pltpu.make_async_copy(vw_hbm, w_buf.at[1], w_sem.at[1]),
    ]
    for copy in w_copies:
        copy.start()
    for copy in in_copies:
        copy.wait()

    ref_rows = n * own
    others = pl.ds(0, (n - 1) * own)
    small = ref_rows <= 256

    def await_rows(c):
        first, count = cuts[c]
        arrived = kv_buf.at[:, others, pl.ds(first * HD, count * HD)]
        pltpu.make_async_copy(arrived, arrived, ag_recv.at[c]).wait()

    starts = [first for first, _ in cuts]
    for g in range(groups):
        cols = pl.ds(g * gw, gw)

        def one_head(head):
            if isinstance(head, int):
                hc = pl.ds(head * HD, HD)
            else:
                hc = pl.ds(pl.multiple_of(head * HD, HD), HD)
            key = kv_buf[0, :, hc]
            value = kv_buf[1, :, hc]
            if small:
                grad_key = grad_value = None
                for lo in range(0, tokens, CHUNK):
                    tok = slice(lo, min(lo + CHUNK, tokens))
                    ds, gk, gv = attend(q_buf[tok, hc], key, value, g_buf[tok, hc])
                    ds_buf[head, :, tok] = ds
                    grad_key = gk if grad_key is None else grad_key + gk
                    grad_value = gv if grad_value is None else grad_value + gv
            else:
                head_acc[...] = jnp.zeros_like(head_acc)

                def chunk(c, carry):
                    tok = pl.ds(pl.multiple_of(c * HD, HD), HD)
                    ds, gk, gv = attend(q_buf[tok, hc], key, value, g_buf[tok, hc])
                    ds_buf[head, :, tok] = ds
                    head_acc[0] += gk
                    head_acc[1] += gv
                    return carry

                lax.fori_loop(0, tokens // HD, chunk, 0)
                grad_key, grad_value = head_acc[0], head_acc[1]
            parts[0, :, hc] = (grad_key * SCALE).astype(BF16)
            parts[1, :, hc] = grad_value.astype(BF16)

        if small:
            for head in range(g * per, (g + 1) * per):
                if head in starts:
                    await_rows(starts.index(head))
                one_head(head)
        else:
            for head in range(g * per, (g + 1) * per):
                if head in starts:
                    await_rows(starts.index(head))
            lax.fori_loop(g * per, (g + 1) * per, lambda h, c: (one_head(h), c)[1], 0)

        def send_parts(k, g=g, cols=cols):
            to = lax.rem(me + k, n)
            pltpu.make_async_remote_copy(
                src_ref=parts.at[:, pl.ds(pl.multiple_of(to * own, own), own), cols],
                dst_ref=got.at[:, pl.ds((k - 1) * own, own), cols],
                send_sem=aa_send,
                recv_sem=aa_recv.at[g],
                device_id={"seq": to},
                device_id_type=MESH,
            ).start()

        each(1, n, send_parts)

    def query_grads(g):
        def one_head(head):
            if isinstance(head, int):
                hc = pl.ds(head * HD, HD)
            else:
                hc = pl.ds(pl.multiple_of(head * HD, HD), HD)
            gq_buf[:, hc] = (dot_tn(ds_buf[head], kv_buf[0, :, hc]) * SCALE).astype(BF16)

        if small:
            for head in range(g * per, (g + 1) * per):
                one_head(head)
        else:
            lax.fori_loop(g * per, (g + 1) * per, lambda h, c: (one_head(h), c)[1], 0)

    for copy in w_copies:
        copy.wait()
    rs_copies = []
    for g in range(groups):
        if g == 0:
            query_grads(g)
        cols = pl.ds(g * gw, gw)
        arrived = got.at[:, :, cols]
        pltpu.make_async_copy(arrived, arrived, aa_recv.at[g]).wait()
        sides = []
        for side in range(2):
            total = parts[side, my_rows, cols].astype(F32)
            if n <= 8:
                for k in range(n - 1):
                    total += got[side, k * own : (k + 1) * own, cols].astype(F32)
            else:
                total = lax.fori_loop(
                    0,
                    n - 1,
                    lambda k, acc: acc
                    + got[side, pl.ds(pl.multiple_of(k * own, own), own), cols].astype(F32),
                    total,
                )
            high = total.astype(BF16)
            low = (total - high.astype(F32)).astype(BF16)
            sides.append(jnp.concatenate([high, low], axis=0))
        for j in range(1, nt + 1):
            to = lax.rem(mt + j, nt)
            wr = pl.ds(pl.multiple_of(to * out_cols, out_cols), out_cols)
            both = dot_nt(sides[0], w_buf[0, wr, cols]) + dot_nt(sides[1], w_buf[1, wr, cols])
            new = both[:own] + both[own:]
            if g:
                new = new + sums[j - 1]
            if g < groups - 1 or j == nt:
                sums[j - 1] = new
            else:
                out_send[j - 1] = new.astype(BF16)
                copy = pltpu.make_async_remote_copy(
                    src_ref=out_send.at[j - 1],
                    dst_ref=out_got.at[j - 1],
                    send_sem=rs_send.at[j - 1],
                    recv_sem=rs_recv.at[j - 1],
                    device_id={"tensor": to},
                    device_id_type=MESH,
                )
                copy.start()
                rs_copies.append(copy)

    for g in range(1, groups):
        query_grads(g)
    sent = kv_buf.at[:, others]
    pltpu.make_async_copy(sent, sent, ag_send).wait()
    pltpu.make_async_copy(got, got, aa_send).wait()
    total = sums[nt - 1]
    for j, copy in enumerate(rs_copies):
        copy.wait_recv()
        total += out_got[j].astype(F32)
    rows_ref[...] = total.astype(BF16)
    for copy in rs_copies:
        copy.wait_send()


def gather_cuts(heads):
    cuts = []
    at = 0
    while at < heads:
        count = min(1 if at < 2 else 2, heads - at)
        cuts.append((at, count))
        at += count
    return cuts


def deliver(gq_ref, rows_ref, gq_out, rows_out, sem):
    part = gq_ref.shape[0] // SPLIT
    copies = [pltpu.make_async_copy(rows_ref, rows_out, sem.at[SPLIT])]
    for i in range(SPLIT):
        rows = pl.ds(i * part, part)
        copies.append(pltpu.make_async_copy(gq_ref.at[rows], gq_out.at[rows], sem.at[i]))
    for copy in copies:
        copy.start()
    for copy in copies:
        copy.wait()


def solution(mesh):
    n, nt = mesh.shape["seq"], mesh.shape["tensor"]

    def shards(queries, ref_keys, ref_values, grad_out, key_weight, value_weight):
        tokens, width = queries.shape
        own = ref_keys.shape[0]
        features = key_weight.shape[0]
        heads = width // HD
        groups = 3 if heads % 3 == 0 else 1
        cuts = gather_cuts(heads)
        out_cols = features // nt
        hbm_spec = pl.BlockSpec(memory_space=pltpu.HBM)
        vmem_spec = pl.BlockSpec(memory_space=pltpu.VMEM)
        dma = pltpu.SemaphoreType.DMA
        held = pl.pallas_call(
            functools.partial(kernel, n, nt, groups, cuts),
            out_shape=(
                pltpu.VMEM((tokens, width), BF16),
                pltpu.VMEM((own, out_cols), BF16),
            ),
            in_specs=[hbm_spec] * 6,
            out_specs=(vmem_spec, vmem_spec),
            scratch_shapes=[
                pltpu.VMEM((tokens, width), BF16),
                pltpu.VMEM((tokens, width), BF16),
                pltpu.VMEM((heads, n * own, tokens), BF16),
                pltpu.VMEM((2, features, width), BF16),
                pltpu.VMEM((2, n * own, width), BF16),
                pltpu.VMEM((2, n * own, width), BF16),
                pltpu.VMEM((2, (n - 1) * own, width), BF16),
                pltpu.VMEM((nt, own, out_cols), F32),
                pltpu.VMEM((nt - 1, own, out_cols), BF16),
                pltpu.VMEM((nt - 1, own, out_cols), BF16),
                pltpu.VMEM((2, n * own, HD), F32),
                dma((2,)),
                dma((2,)),
                dma((2,)),
                dma,
                dma((len(cuts),)),
                dma,
                dma((groups,)),
                dma((nt - 1,)),
                dma((nt - 1,)),
            ],
            compiler_params=pltpu.CompilerParams(
                collective_id=0,
                has_side_effects=True,
                vmem_limit_bytes=VMEM_LIMIT,
            ),
            cost_estimate=pl.CostEstimate(
                flops=1_000_000_000, bytes_accessed=12_000_000, transcendentals=400_000
            ),
        )(
            *(
                pltpu.with_memory_space_constraint(x, pltpu.HBM)
                for x in (queries, ref_keys, ref_values, grad_out, key_weight, value_weight)
            )
        )
        return pl.pallas_call(
            deliver,
            out_shape=(
                jax.ShapeDtypeStruct((tokens, width), BF16),
                jax.ShapeDtypeStruct((own, out_cols), BF16),
            ),
            in_specs=[vmem_spec] * 2,
            out_specs=(hbm_spec, hbm_spec),
            scratch_shapes=[dma((SPLIT + 1,))],
        )(*(pltpu.with_memory_space_constraint(x, pltpu.VMEM) for x in held))

    placed = (
        P("seq", "tensor"),
        P("seq", "tensor"),
        P("seq", "tensor"),
        P("seq", "tensor"),
        P(None, "tensor"),
        P(None, "tensor"),
    )
    return jax.shard_map(
        shards,
        mesh=mesh,
        in_specs=placed,
        out_specs=(P("seq", "tensor"), P("seq", "tensor")),
        check_vma=False,
    )
```

```python
import functools
import math

import jax
import jax.numpy as jnp
from jax import lax
from jax.experimental import pallas as pl
from jax.experimental.pallas import tpu as pltpu
from jax.sharding import PartitionSpec as P

HD = 128
CHUNK = 256
SPLIT = 4
VMEM_LIMIT = 48 * 1024 * 1024
SCALE = 1.0 / HD**0.5
EXP_SCALE = SCALE * math.log2(math.e)
MESH = pl.DeviceIdType.MESH
F32 = jnp.float32
BF16 = jnp.bfloat16


def each(lo, hi, body):
    if hi - lo <= 8:
        for i in range(lo, hi):
            body(i)
    else:

        def step(i, carry):
            body(i)
            return carry

        lax.fori_loop(lo, hi, step, 0)


def dot_nt(a, b):
    return lax.dot_general(a, b, (((1,), (1,)), ((), ())), preferred_element_type=F32)


def dot_tn(a, b):
    return lax.dot_general(a, b, (((0,), (0,)), ((), ())), preferred_element_type=F32)


def dot_nn(a, b):
    return jnp.dot(a, b, preferred_element_type=F32)


def attend(query, key, value, grad):
    scores = dot_nt(key, query)
    grad_probs = dot_nt(value, grad)
    top = jnp.max(scores, axis=0, keepdims=True)
    weights = jnp.exp2((scores - top) * EXP_SCALE)
    inverse = 1.0 / jnp.sum(weights, axis=0, keepdims=True)
    probs = weights * inverse
    delta = jnp.sum(probs * grad_probs, axis=0, keepdims=True)
    grad_scores = (probs * (grad_probs - delta)).astype(BF16)
    grad_key = dot_nn(grad_scores, query)
    grad_value = dot_nn(probs.astype(BF16), grad)
    return grad_scores, grad_key, grad_value


def kernel(
    n,
    nt,
    groups,
    cuts,
    q_hbm,
    k_hbm,
    v_hbm,
    g_hbm,
    kw_hbm,
    vw_hbm,
    gq_buf,
    rows_ref,
    q_buf,
    g_buf,
    ds_buf,
    w_buf,
    kv_buf,
    parts,
    got,
    sums,
    rest,
    out_send,
    out_got,
    head_acc,
    in_sem,
    own_sem,
    w_sem,
    ag_send,
    ag_recv,
    aa_send,
    aa_recv,
    rs_send,
    rs_recv,
):
    me = lax.axis_index("seq")
    mt = lax.axis_index("tensor")
    tokens, width = q_hbm.shape
    own = k_hbm.shape[0]
    heads = width // HD
    per = heads // groups
    gw = per * HD
    out_cols = rows_ref.shape[1]
    my_rows = pl.ds(pl.multiple_of(me * own, own), own)

    barrier = pltpu.get_barrier_semaphore()

    def greet_seq(k):
        pl.semaphore_signal(
            barrier, inc=1, device_id={"seq": lax.rem(me + k, n)}, device_id_type=MESH
        )

    def greet_tensor(k):
        pl.semaphore_signal(
            barrier, inc=1, device_id={"tensor": lax.rem(mt + k, nt)}, device_id_type=MESH
        )

    each(1, n, greet_seq)
    each(1, nt, greet_tensor)
    own_copies = [
        pltpu.make_async_copy(k_hbm, kv_buf.at[0, my_rows], own_sem.at[0]),
        pltpu.make_async_copy(v_hbm, kv_buf.at[1, my_rows], own_sem.at[1]),
    ]
    for copy in own_copies:
        copy.start()
    in_copies = [
        pltpu.make_async_copy(q_hbm, q_buf, in_sem.at[0]),
        pltpu.make_async_copy(g_hbm, g_buf, in_sem.at[1]),
    ]
    for copy in in_copies:
        copy.start()

    for copy in own_copies:
        copy.wait()
    pl.semaphore_wait(barrier, n + nt - 2)

    for c, (first, count) in enumerate(cuts):
        cols = pl.ds(first * HD, count * HD)

        def send_rows(k, c=c, cols=cols):
            block = kv_buf.at[:, my_rows, cols]
            pltpu.make_async_remote_copy(
                src_ref=block,
                dst_ref=block,
                send_sem=ag_send,
                recv_sem=ag_recv.at[c],
                device_id={"seq": lax.rem(me + k, n)},
                device_id_type=MESH,
            ).start()

        each(1, n, send_rows)

    w_copies = [
        pltpu.make_async_copy(kw_hbm, w_buf.at[0], w_sem.at[0]),
        pltpu.make_async_copy(vw_hbm, w_buf.at[1], w_sem.at[1]),
    ]
    for copy in w_copies:
        copy.start()
    for copy in in_copies:
        copy.wait()

    ref_rows = n * own
    others = pl.ds(0, (n - 1) * own)
    small = ref_rows <= 256

    def await_rows(c):
        first, count = cuts[c]
        arrived = kv_buf.at[:, others, pl.ds(first * HD, count * HD)]
        pltpu.make_async_copy(arrived, arrived, ag_recv.at[c]).wait()

    starts = [first for first, _ in cuts]
    for g in range(groups):
        cols = pl.ds(g * gw, gw)

        def one_head(head):
            if isinstance(head, int):
                hc = pl.ds(head * HD, HD)
            else:
                hc = pl.ds(pl.multiple_of(head * HD, HD), HD)
            key = kv_buf[0, :, hc]
            value = kv_buf[1, :, hc]
            if small:
                grad_key = grad_value = None
                for lo in range(0, tokens, CHUNK):
                    tok = slice(lo, min(lo + CHUNK, tokens))
                    ds, gk, gv = attend(q_buf[tok, hc], key, value, g_buf[tok, hc])
                    ds_buf[head, :, tok] = ds
                    grad_key = gk if grad_key is None else grad_key + gk
                    grad_value = gv if grad_value is None else grad_value + gv
            else:
                head_acc[...] = jnp.zeros_like(head_acc)

                def chunk(c, carry):
                    tok = pl.ds(pl.multiple_of(c * HD, HD), HD)
                    ds, gk, gv = attend(q_buf[tok, hc], key, value, g_buf[tok, hc])
                    ds_buf[head, :, tok] = ds
                    head_acc[0] += gk
                    head_acc[1] += gv
                    return carry

                lax.fori_loop(0, tokens // HD, chunk, 0)
                grad_key, grad_value = head_acc[0], head_acc[1]
            parts[0, :, hc] = (grad_key * SCALE).astype(BF16)
            parts[1, :, hc] = grad_value.astype(BF16)

        if small:
            for head in range(g * per, (g + 1) * per):
                if head in starts:
                    await_rows(starts.index(head))
                one_head(head)
        else:
            for head in range(g * per, (g + 1) * per):
                if head in starts:
                    await_rows(starts.index(head))
            lax.fori_loop(g * per, (g + 1) * per, lambda h, c: (one_head(h), c)[1], 0)

        def send_parts(k, g=g, cols=cols):
            to = lax.rem(me + k, n)
            pltpu.make_async_remote_copy(
                src_ref=parts.at[:, pl.ds(pl.multiple_of(to * own, own), own), cols],
                dst_ref=got.at[:, pl.ds((k - 1) * own, own), cols],
                send_sem=aa_send,
                recv_sem=aa_recv.at[g],
                device_id={"seq": to},
                device_id_type=MESH,
            ).start()

        each(1, n, send_parts)

    def query_grads(g):
        def one_head(head):
            if isinstance(head, int):
                hc = pl.ds(head * HD, HD)
            else:
                hc = pl.ds(pl.multiple_of(head * HD, HD), HD)
            gq_buf[:, hc] = (dot_tn(ds_buf[head], kv_buf[0, :, hc]) * SCALE).astype(BF16)

        if small:
            for head in range(g * per, (g + 1) * per):
                one_head(head)
        else:
            lax.fori_loop(g * per, (g + 1) * per, lambda h, c: (one_head(h), c)[1], 0)

    for copy in w_copies:
        copy.wait()
    rs_copies = []
    query_grads(0)
    steps = [(0, groups - 1), (groups - 1, groups)] if groups > 1 else [(0, 1)]
    for lo, hi in steps:
        cols = pl.ds(lo * gw, (hi - lo) * gw)
        for g in range(lo, hi):
            arrived = got.at[:, :, pl.ds(g * gw, gw)]
            pltpu.make_async_copy(arrived, arrived, aa_recv.at[g]).wait()
        sides = []
        for side in range(2):
            total = parts[side, my_rows, cols].astype(F32)
            if n <= 8:
                for k in range(n - 1):
                    total += got[side, k * own : (k + 1) * own, cols].astype(F32)
            else:
                total = lax.fori_loop(
                    0,
                    n - 1,
                    lambda k, acc: acc
                    + got[side, pl.ds(pl.multiple_of(k * own, own), own), cols].astype(F32),
                    total,
                )
            high = total.astype(BF16)
            low = (total - high.astype(F32)).astype(BF16)
            sides.append(jnp.concatenate([high, low], axis=0))
        for j in range(1, nt + 1):
            to = lax.rem(mt + j, nt)
            wr = pl.ds(pl.multiple_of(to * out_cols, out_cols), out_cols)
            new = dot_nt(w_buf[0, wr, cols], sides[0]) + dot_nt(w_buf[1, wr, cols], sides[1])
            if lo:
                new = new + sums[j - 1]
            if hi < groups:
                sums[j - 1] = new
                continue
            both = new.T
            block = both[:own] + both[own:]
            if j == nt:
                rest[...] = block
            else:
                out_send[j - 1] = block.astype(BF16)
                copy = pltpu.make_async_remote_copy(
                    src_ref=out_send.at[j - 1],
                    dst_ref=out_got.at[j - 1],
                    send_sem=rs_send.at[j - 1],
                    recv_sem=rs_recv.at[j - 1],
                    device_id={"tensor": to},
                    device_id_type=MESH,
                )
                copy.start()
                rs_copies.append(copy)

    for g in range(1, groups):
        query_grads(g)
    sent = kv_buf.at[:, others]
    pltpu.make_async_copy(sent, sent, ag_send).wait()
    pltpu.make_async_copy(got, got, aa_send).wait()
    total = rest[...]
    for j, copy in enumerate(rs_copies):
        copy.wait_recv()
        total += out_got[j].astype(F32)
    rows_ref[...] = total.astype(BF16)
    for copy in rs_copies:
        copy.wait_send()


def gather_cuts(heads):
    cuts = []
    at = 0
    while at < heads:
        count = min(1 if at < 2 else 2, heads - at)
        cuts.append((at, count))
        at += count
    return cuts


def deliver(gq_ref, rows_ref, gq_out, rows_out, sem):
    part = gq_ref.shape[0] // SPLIT
    copies = [pltpu.make_async_copy(rows_ref, rows_out, sem.at[SPLIT])]
    for i in range(SPLIT):
        rows = pl.ds(i * part, part)
        copies.append(pltpu.make_async_copy(gq_ref.at[rows], gq_out.at[rows], sem.at[i]))
    for copy in copies:
        copy.start()
    for copy in copies:
        copy.wait()


def solution(mesh):
    n, nt = mesh.shape["seq"], mesh.shape["tensor"]

    def shards(queries, ref_keys, ref_values, grad_out, key_weight, value_weight):
        tokens, width = queries.shape
        own = ref_keys.shape[0]
        features = key_weight.shape[0]
        heads = width // HD
        groups = 3 if heads % 3 == 0 else 1
        cuts = gather_cuts(heads)
        out_cols = features // nt
        hbm_spec = pl.BlockSpec(memory_space=pltpu.HBM)
        vmem_spec = pl.BlockSpec(memory_space=pltpu.VMEM)
        dma = pltpu.SemaphoreType.DMA
        held = pl.pallas_call(
            functools.partial(kernel, n, nt, groups, cuts),
            out_shape=(
                pltpu.VMEM((tokens, width), BF16),
                pltpu.VMEM((own, out_cols), BF16),
            ),
            in_specs=[hbm_spec] * 6,
            out_specs=(vmem_spec, vmem_spec),
            scratch_shapes=[
                pltpu.VMEM((tokens, width), BF16),
                pltpu.VMEM((tokens, width), BF16),
                pltpu.VMEM((heads, n * own, tokens), BF16),
                pltpu.VMEM((2, features, width), BF16),
                pltpu.VMEM((2, n * own, width), BF16),
                pltpu.VMEM((2, n * own, width), BF16),
                pltpu.VMEM((2, (n - 1) * own, width), BF16),
                pltpu.VMEM((nt, out_cols, 2 * own), F32),
                pltpu.VMEM((own, out_cols), F32),
                pltpu.VMEM((nt - 1, own, out_cols), BF16),
                pltpu.VMEM((nt - 1, own, out_cols), BF16),
                pltpu.VMEM((2, n * own, HD), F32),
                dma((2,)),
                dma((2,)),
                dma((2,)),
                dma,
                dma((len(cuts),)),
                dma,
                dma((groups,)),
                dma((nt - 1,)),
                dma((nt - 1,)),
            ],
            compiler_params=pltpu.CompilerParams(
                collective_id=0,
                has_side_effects=True,
                vmem_limit_bytes=VMEM_LIMIT,
            ),
            cost_estimate=pl.CostEstimate(
                flops=1_000_000_000, bytes_accessed=12_000_000, transcendentals=400_000
            ),
        )(
            *(
                pltpu.with_memory_space_constraint(x, pltpu.HBM)
                for x in (queries, ref_keys, ref_values, grad_out, key_weight, value_weight)
            )
        )
        return pl.pallas_call(
            deliver,
            out_shape=(
                jax.ShapeDtypeStruct((tokens, width), BF16),
                jax.ShapeDtypeStruct((own, out_cols), BF16),
            ),
            in_specs=[vmem_spec] * 2,
            out_specs=(hbm_spec, hbm_spec),
            scratch_shapes=[dma((SPLIT + 1,))],
        )(*(pltpu.with_memory_space_constraint(x, pltpu.VMEM) for x in held))

    placed = (
        P("seq", "tensor"),
        P("seq", "tensor"),
        P("seq", "tensor"),
        P("seq", "tensor"),
        P(None, "tensor"),
        P(None, "tensor"),
    )
    return jax.shard_map(
        shards,
        mesh=mesh,
        in_specs=placed,
        out_specs=(P("seq", "tensor"), P("seq", "tensor")),
        check_vma=False,
    )
```

```python
import functools
import math

import jax
import jax.numpy as jnp
from jax import lax
from jax.experimental import pallas as pl
from jax.experimental.pallas import tpu as pltpu
from jax.sharding import PartitionSpec as P

HD = 128
CHUNK = 256
SPLIT = 4
VMEM_LIMIT = 48 * 1024 * 1024
SCALE = 1.0 / HD**0.5
EXP_SCALE = SCALE * math.log2(math.e)
MESH = pl.DeviceIdType.MESH
F32 = jnp.float32
BF16 = jnp.bfloat16


def each(lo, hi, body):
    if hi - lo <= 8:
        for i in range(lo, hi):
            body(i)
    else:

        def step(i, carry):
            body(i)
            return carry

        lax.fori_loop(lo, hi, step, 0)


def dot_nt(a, b):
    return lax.dot_general(a, b, (((1,), (1,)), ((), ())), preferred_element_type=F32)


def dot_tn(a, b):
    return lax.dot_general(a, b, (((0,), (0,)), ((), ())), preferred_element_type=F32)


def dot_nn(a, b):
    return jnp.dot(a, b, preferred_element_type=F32)


def attend(query, key, value, grad):
    scores = dot_nt(key, query)
    grad_probs = dot_nt(value, grad)
    top = jnp.max(scores, axis=0, keepdims=True)
    weights = jnp.exp2((scores - top) * EXP_SCALE)
    inverse = 1.0 / jnp.sum(weights, axis=0, keepdims=True)
    probs = weights * inverse
    delta = jnp.sum(probs * grad_probs, axis=0, keepdims=True)
    grad_scores = (probs * (grad_probs - delta)).astype(BF16)
    grad_key = dot_nn(grad_scores, query)
    grad_value = dot_nn(probs.astype(BF16), grad)
    return grad_scores, grad_key, grad_value


def kernel(
    n,
    nt,
    groups,
    cuts,
    q_hbm,
    k_hbm,
    v_hbm,
    g_hbm,
    kw_hbm,
    vw_hbm,
    gq_buf,
    rows_ref,
    q_buf,
    g_buf,
    ds_buf,
    w_buf,
    kv_buf,
    parts,
    mate_got,
    pair_buf,
    got,
    sums,
    rest,
    out_send,
    out_got,
    head_acc,
    in_sem,
    own_sem,
    w_sem,
    ag_send,
    ag_recv,
    fw_send,
    fw_recv,
    sw_send,
    sw_recv,
    aa_send,
    aa_recv,
    rs_send,
    rs_recv,
):
    me = lax.axis_index("seq")
    mt = lax.axis_index("tensor")
    tokens, width = q_hbm.shape
    own = k_hbm.shape[0]
    heads = width // HD
    per = heads // groups
    gw = per * HD
    out_cols = rows_ref.shape[1]
    pairs = n // 2
    half = pairs * own
    parity = lax.rem(me, 2)
    mine = me // 2
    mate = me + 1 - 2 * parity
    my_at = pl.multiple_of(parity * half, half)
    mate_at = pl.multiple_of((1 - parity) * half, half)
    pair_rows = pl.ds(pl.multiple_of(mine * own, own), own)
    my_rows = pl.ds(pl.multiple_of(my_at + mine * own, own), own)

    barrier = pltpu.get_barrier_semaphore()

    def peer(k):
        return 2 * lax.rem(mine + k, pairs) + parity

    def greet_seq(k):
        pl.semaphore_signal(barrier, inc=1, device_id={"seq": peer(k)}, device_id_type=MESH)

    def greet_tensor(k):
        pl.semaphore_signal(
            barrier, inc=1, device_id={"tensor": lax.rem(mt + k, nt)}, device_id_type=MESH
        )

    each(1, pairs, greet_seq)
    pl.semaphore_signal(barrier, inc=1, device_id={"seq": mate}, device_id_type=MESH)
    each(1, nt, greet_tensor)
    own_copies = [
        pltpu.make_async_copy(k_hbm, kv_buf.at[0, my_rows], own_sem.at[0]),
        pltpu.make_async_copy(v_hbm, kv_buf.at[1, my_rows], own_sem.at[1]),
    ]
    for copy in own_copies:
        copy.start()
    in_copies = [
        pltpu.make_async_copy(q_hbm, q_buf, in_sem.at[0]),
        pltpu.make_async_copy(g_hbm, g_buf, in_sem.at[1]),
    ]
    for copy in in_copies:
        copy.start()

    for copy in own_copies:
        copy.wait()
    pl.semaphore_wait(barrier, pairs + nt - 1)

    for c, (first, count) in enumerate(cuts):
        cols = pl.ds(first * HD, count * HD)

        def send_rows(k, c=c, cols=cols):
            block = kv_buf.at[:, my_rows, cols]
            pltpu.make_async_remote_copy(
                src_ref=block,
                dst_ref=block,
                send_sem=ag_send,
                recv_sem=ag_recv.at[c],
                device_id={"seq": peer(k)},
                device_id_type=MESH,
            ).start()

        each(1, pairs, send_rows)

    w_copies = [
        pltpu.make_async_copy(kw_hbm, w_buf.at[0], w_sem.at[0]),
        pltpu.make_async_copy(vw_hbm, w_buf.at[1], w_sem.at[1]),
    ]
    for copy in w_copies:
        copy.start()
    for copy in in_copies:
        copy.wait()

    ref_rows = n * own
    others = pl.ds(0, half - own)
    small = ref_rows <= 256

    def to_mate(src, dst, send_sem, recv_sem):
        return pltpu.make_async_remote_copy(
            src_ref=src,
            dst_ref=dst,
            send_sem=send_sem,
            recv_sem=recv_sem,
            device_id={"seq": mate},
            device_id_type=MESH,
        )

    def forward_rows(c):
        first, count = cuts[c]
        cols = pl.ds(first * HD, count * HD)
        arrived = kv_buf.at[:, others, cols]
        pltpu.make_async_copy(arrived, arrived, ag_recv.at[c]).wait()
        block = kv_buf.at[:, pl.ds(my_at, half), cols]
        copy = to_mate(block, block, fw_send.at[c], fw_recv.at[c])
        copy.start()
        forwards.append(copy)

    def await_rows(c):
        if c + 1 < len(cuts):
            forward_rows(c + 1)
        forwards[c].wait_recv()

    def send_pair_sums(g):
        cols = pl.ds(g * gw, gw)
        swaps[g].wait_recv()
        for side in range(2):
            both = parts[side, pl.ds(my_at, half), cols].astype(F32)
            both += mate_got[side, :, cols].astype(F32)
            pair_buf[side, :, cols] = both.astype(BF16)

        def send_one(k):
            to = lax.rem(mine + k, pairs)
            pltpu.make_async_remote_copy(
                src_ref=pair_buf.at[:, pl.ds(pl.multiple_of(to * own, own), own), cols],
                dst_ref=got.at[:, pl.ds((k - 1) * own, own), cols],
                send_sem=aa_send,
                recv_sem=aa_recv.at[g],
                device_id={"seq": 2 * to + parity},
                device_id_type=MESH,
            ).start()

        each(1, pairs, send_one)

    forwards = []
    swaps = []
    forward_rows(0)
    starts = [first for first, _ in cuts]
    for g in range(groups):
        cols = pl.ds(g * gw, gw)

        def one_head(head):
            if isinstance(head, int):
                hc = pl.ds(head * HD, HD)
            else:
                hc = pl.ds(pl.multiple_of(head * HD, HD), HD)
            key = kv_buf[0, :, hc]
            value = kv_buf[1, :, hc]
            if small:
                grad_key = grad_value = None
                for lo in range(0, tokens, CHUNK):
                    tok = slice(lo, min(lo + CHUNK, tokens))
                    ds, gk, gv = attend(q_buf[tok, hc], key, value, g_buf[tok, hc])
                    ds_buf[head, :, tok] = ds
                    grad_key = gk if grad_key is None else grad_key + gk
                    grad_value = gv if grad_value is None else grad_value + gv
            else:
                head_acc[...] = jnp.zeros_like(head_acc)

                def chunk(c, carry):
                    tok = pl.ds(pl.multiple_of(c * HD, HD), HD)
                    ds, gk, gv = attend(q_buf[tok, hc], key, value, g_buf[tok, hc])
                    ds_buf[head, :, tok] = ds
                    head_acc[0] += gk
                    head_acc[1] += gv
                    return carry

                lax.fori_loop(0, tokens // HD, chunk, 0)
                grad_key, grad_value = head_acc[0], head_acc[1]
            parts[0, :, hc] = (grad_key * SCALE).astype(BF16)
            parts[1, :, hc] = grad_value.astype(BF16)

        if small:
            for head in range(g * per, (g + 1) * per):
                if head in starts:
                    await_rows(starts.index(head))
                one_head(head)
        else:
            for head in range(g * per, (g + 1) * per):
                if head in starts:
                    await_rows(starts.index(head))
            lax.fori_loop(g * per, (g + 1) * per, lambda h, c: (one_head(h), c)[1], 0)

        swap = to_mate(
            parts.at[:, pl.ds(mate_at, half), cols],
            mate_got.at[:, :, cols],
            sw_send.at[g],
            sw_recv.at[g],
        )
        swap.start()
        swaps.append(swap)
        if g:
            send_pair_sums(g - 1)

    def query_grads(g):
        def one_head(head):
            if isinstance(head, int):
                hc = pl.ds(head * HD, HD)
            else:
                hc = pl.ds(pl.multiple_of(head * HD, HD), HD)
            gq_buf[:, hc] = (dot_tn(ds_buf[head], kv_buf[0, :, hc]) * SCALE).astype(BF16)

        if small:
            for head in range(g * per, (g + 1) * per):
                one_head(head)
        else:
            lax.fori_loop(g * per, (g + 1) * per, lambda h, c: (one_head(h), c)[1], 0)

    rs_copies = []
    query_grads(0)
    send_pair_sums(groups - 1)
    for copy in w_copies:
        copy.wait()
    steps = [(0, groups - 1), (groups - 1, groups)] if groups > 1 else [(0, 1)]
    for lo, hi in steps:
        cols = pl.ds(lo * gw, (hi - lo) * gw)
        for g in range(lo, hi):
            arrived = got.at[:, :, pl.ds(g * gw, gw)]
            pltpu.make_async_copy(arrived, arrived, aa_recv.at[g]).wait()
        sides = []
        for side in range(2):
            total = parts[side, my_rows, cols].astype(F32)
            total += mate_got[side, pair_rows, cols].astype(F32)
            if n <= 8:
                for k in range(pairs - 1):
                    total += got[side, k * own : (k + 1) * own, cols].astype(F32)
            else:
                total = lax.fori_loop(
                    0,
                    pairs - 1,
                    lambda k, acc: acc
                    + got[side, pl.ds(pl.multiple_of(k * own, own), own), cols].astype(F32),
                    total,
                )
            high = total.astype(BF16)
            low = (total - high.astype(F32)).astype(BF16)
            sides.append(jnp.concatenate([high, low], axis=0))
        for j in range(1, nt + 1):
            to = lax.rem(mt + j, nt)
            wr = pl.ds(pl.multiple_of(to * out_cols, out_cols), out_cols)
            both = dot_nt(sides[0], w_buf[0, wr, cols]) + dot_nt(sides[1], w_buf[1, wr, cols])
            block = both[:own] + both[own:]
            if lo:
                block = block + sums[j - 1]
            if hi < groups:
                sums[j - 1] = block
                continue
            if j == nt:
                rest[...] = block
            else:
                out_send[j - 1] = block.astype(BF16)
                copy = pltpu.make_async_remote_copy(
                    src_ref=out_send.at[j - 1],
                    dst_ref=out_got.at[j - 1],
                    send_sem=rs_send.at[j - 1],
                    recv_sem=rs_recv.at[j - 1],
                    device_id={"tensor": to},
                    device_id_type=MESH,
                )
                copy.start()
                rs_copies.append(copy)

    for g in range(1, groups):
        query_grads(g)
    sent = kv_buf.at[:, others]
    pltpu.make_async_copy(sent, sent, ag_send).wait()
    pltpu.make_async_copy(got, got, aa_send).wait()
    for copy in forwards + swaps:
        copy.wait_send()
    total = rest[...]
    for j, copy in enumerate(rs_copies):
        copy.wait_recv()
        total += out_got[j].astype(F32)
    rows_ref[...] = total.astype(BF16)
    for copy in rs_copies:
        copy.wait_send()


def deliver(gq_ref, rows_ref, gq_out, rows_out, sem):
    part = gq_ref.shape[0] // SPLIT
    copies = [pltpu.make_async_copy(rows_ref, rows_out, sem.at[SPLIT])]
    for i in range(SPLIT):
        rows = pl.ds(i * part, part)
        copies.append(pltpu.make_async_copy(gq_ref.at[rows], gq_out.at[rows], sem.at[i]))
    for copy in copies:
        copy.start()
    for copy in copies:
        copy.wait()


def solution(mesh):
    n, nt = mesh.shape["seq"], mesh.shape["tensor"]

    def shards(queries, ref_keys, ref_values, grad_out, key_weight, value_weight):
        tokens, width = queries.shape
        own = ref_keys.shape[0]
        features = key_weight.shape[0]
        heads = width // HD
        groups = 3 if heads % 3 == 0 else 1
        per = heads // groups
        cuts = [(g * per, per) for g in range(groups)]
        out_cols = features // nt
        hbm_spec = pl.BlockSpec(memory_space=pltpu.HBM)
        vmem_spec = pl.BlockSpec(memory_space=pltpu.VMEM)
        dma = pltpu.SemaphoreType.DMA
        held = pl.pallas_call(
            functools.partial(kernel, n, nt, groups, cuts),
            out_shape=(
                pltpu.VMEM((tokens, width), BF16),
                pltpu.VMEM((own, out_cols), BF16),
            ),
            in_specs=[hbm_spec] * 6,
            out_specs=(vmem_spec, vmem_spec),
            scratch_shapes=[
                pltpu.VMEM((tokens, width), BF16),
                pltpu.VMEM((tokens, width), BF16),
                pltpu.VMEM((heads, n * own, tokens), BF16),
                pltpu.VMEM((2, features, width), BF16),
                pltpu.VMEM((2, n * own, width), BF16),
                pltpu.VMEM((2, n * own, width), BF16),
                pltpu.VMEM((2, n // 2 * own, width), BF16),
                pltpu.VMEM((2, n // 2 * own, width), BF16),
                pltpu.VMEM((2, (n // 2 - 1) * own, width), BF16),
                pltpu.VMEM((nt, own, out_cols), F32),
                pltpu.VMEM((own, out_cols), F32),
                pltpu.VMEM((nt - 1, own, out_cols), BF16),
                pltpu.VMEM((nt - 1, own, out_cols), BF16),
                pltpu.VMEM((2, n * own, HD), F32),
                dma((2,)),
                dma((2,)),
                dma((2,)),
                dma,
                dma((len(cuts),)),
                dma((len(cuts),)),
                dma((len(cuts),)),
                dma((groups,)),
                dma((groups,)),
                dma,
                dma((groups,)),
                dma((nt - 1,)),
                dma((nt - 1,)),
            ],
            compiler_params=pltpu.CompilerParams(
                collective_id=0,
                has_side_effects=True,
                vmem_limit_bytes=VMEM_LIMIT,
            ),
            cost_estimate=pl.CostEstimate(
                flops=1_000_000_000, bytes_accessed=12_000_000, transcendentals=400_000
            ),
        )(
            *(
                pltpu.with_memory_space_constraint(x, pltpu.HBM)
                for x in (queries, ref_keys, ref_values, grad_out, key_weight, value_weight)
            )
        )
        return pl.pallas_call(
            deliver,
            out_shape=(
                jax.ShapeDtypeStruct((tokens, width), BF16),
                jax.ShapeDtypeStruct((own, out_cols), BF16),
            ),
            in_specs=[vmem_spec] * 2,
            out_specs=(hbm_spec, hbm_spec),
            scratch_shapes=[dma((SPLIT + 1,))],
        )(*(pltpu.with_memory_space_constraint(x, pltpu.VMEM) for x in held))

    placed = (
        P("seq", "tensor"),
        P("seq", "tensor"),
        P("seq", "tensor"),
        P("seq", "tensor"),
        P(None, "tensor"),
        P(None, "tensor"),
    )
    return jax.shard_map(
        shards,
        mesh=mesh,
        in_specs=placed,
        out_specs=(P("seq", "tensor"), P("seq", "tensor")),
        check_vma=False,
    )
```

```python
import functools
import math

import jax
import jax.numpy as jnp
from jax import lax
from jax.experimental import pallas as pl
from jax.experimental.pallas import tpu as pltpu
from jax.sharding import PartitionSpec as P

HD = 128
CHUNK = 256
SPLIT = 4
VMEM_LIMIT = 48 * 1024 * 1024
SCALE = 1.0 / HD**0.5
EXP_SCALE = SCALE * math.log2(math.e)
MESH = pl.DeviceIdType.MESH
F32 = jnp.float32
BF16 = jnp.bfloat16


def each(lo, hi, body):
    if hi - lo <= 8:
        for i in range(lo, hi):
            body(i)
    else:

        def step(i, carry):
            body(i)
            return carry

        lax.fori_loop(lo, hi, step, 0)


def dot_nt(a, b):
    return lax.dot_general(a, b, (((1,), (1,)), ((), ())), preferred_element_type=F32)


def dot_tn(a, b):
    return lax.dot_general(a, b, (((0,), (0,)), ((), ())), preferred_element_type=F32)


def dot_nn(a, b):
    return jnp.dot(a, b, preferred_element_type=F32)


def score(query, key, value, grad):
    return dot_nt(key, query), dot_nt(value, grad)


def soften(scores, grad_probs):
    top = jnp.max(scores, axis=0, keepdims=True)
    weights = jnp.exp2((scores - top) * EXP_SCALE)
    inverse = 1.0 / jnp.sum(weights, axis=0, keepdims=True)
    probs = weights * inverse
    delta = jnp.sum(probs * grad_probs, axis=0, keepdims=True)
    grad_scores = (probs * (grad_probs - delta)).astype(BF16)
    return grad_scores, probs.astype(BF16)


def attend(query, key, value, grad):
    grad_scores, probs = soften(*score(query, key, value, grad))
    return grad_scores, dot_nn(grad_scores, query), dot_nn(probs, grad)


def kernel(
    n,
    nt,
    groups,
    cuts,
    q_hbm,
    k_hbm,
    v_hbm,
    g_hbm,
    kw_hbm,
    vw_hbm,
    gq_buf,
    rows_ref,
    q_buf,
    g_buf,
    ds_buf,
    w_buf,
    kv_buf,
    parts,
    got,
    sums,
    out_send,
    out_got,
    head_acc,
    in_sem,
    own_sem,
    w_sem,
    ag_send,
    ag_recv,
    aa_send,
    aa_recv,
    rs_send,
    rs_recv,
):
    me = lax.axis_index("seq")
    mt = lax.axis_index("tensor")
    tokens, width = q_hbm.shape
    own = k_hbm.shape[0]
    heads = width // HD
    per = heads // groups
    gw = per * HD
    out_cols = rows_ref.shape[1]
    my_rows = pl.ds(pl.multiple_of(me * own, own), own)

    barrier = pltpu.get_barrier_semaphore()

    def greet_seq(k):
        pl.semaphore_signal(
            barrier, inc=1, device_id={"seq": lax.rem(me + k, n)}, device_id_type=MESH
        )

    def greet_tensor(k):
        pl.semaphore_signal(
            barrier, inc=1, device_id={"tensor": lax.rem(mt + k, nt)}, device_id_type=MESH
        )

    each(1, n, greet_seq)
    each(1, nt, greet_tensor)
    own_copies = [
        pltpu.make_async_copy(k_hbm, kv_buf.at[0, my_rows], own_sem.at[0]),
        pltpu.make_async_copy(v_hbm, kv_buf.at[1, my_rows], own_sem.at[1]),
    ]
    for copy in own_copies:
        copy.start()
    in_copies = [
        pltpu.make_async_copy(q_hbm, q_buf, in_sem.at[0]),
        pltpu.make_async_copy(g_hbm, g_buf, in_sem.at[1]),
    ]
    for copy in in_copies:
        copy.start()

    for copy in own_copies:
        copy.wait()
    pl.semaphore_wait(barrier, n + nt - 2)

    for c, (first, count) in enumerate(cuts):
        cols = pl.ds(first * HD, count * HD)

        def send_rows(k, c=c, cols=cols):
            block = kv_buf.at[:, my_rows, cols]
            pltpu.make_async_remote_copy(
                src_ref=block,
                dst_ref=block,
                send_sem=ag_send,
                recv_sem=ag_recv.at[c],
                device_id={"seq": lax.rem(me + k, n)},
                device_id_type=MESH,
            ).start()

        each(1, n, send_rows)

    w_copies = []
    for b in range(nt):
        wr = pl.ds(b * out_cols, out_cols)
        for side, ref in enumerate((kw_hbm, vw_hbm)):
            w_copies.append(
                pltpu.make_async_copy(ref.at[wr], w_buf.at[side, wr], w_sem.at[side, b])
            )
    for copy in w_copies:
        copy.start()
    for copy in in_copies:
        copy.wait()

    ref_rows = n * own
    others = pl.ds(0, (n - 1) * own)
    small = ref_rows <= 256

    def await_rows(c):
        first, count = cuts[c]
        arrived = kv_buf.at[:, others, pl.ds(first * HD, count * HD)]
        pltpu.make_async_copy(arrived, arrived, ag_recv.at[c]).wait()

    starts = [first for first, _ in cuts]
    for g in range(groups):
        cols = pl.ds(g * gw, gw)

        def one_head(head):
            if isinstance(head, int):
                hc = pl.ds(head * HD, HD)
            else:
                hc = pl.ds(pl.multiple_of(head * HD, HD), HD)
            key = kv_buf[0, :, hc]
            value = kv_buf[1, :, hc]
            head_acc[...] = jnp.zeros_like(head_acc)

            def chunk(c, carry):
                tok = pl.ds(pl.multiple_of(c * HD, HD), HD)
                ds, gk, gv = attend(q_buf[tok, hc], key, value, g_buf[tok, hc])
                ds_buf[head, :, tok] = ds
                head_acc[0] += gk
                head_acc[1] += gv
                return carry

            lax.fori_loop(0, tokens // HD, chunk, 0)
            grad_key, grad_value = head_acc[0], head_acc[1]
            parts[0, :, hc] = (grad_key * SCALE).astype(BF16)
            parts[1, :, hc] = grad_value.astype(BF16)

        if small:
            units = [
                (head, slice(lo, min(lo + CHUNK, tokens)))
                for head in range(g * per, (g + 1) * per)
                for lo in range(0, tokens, CHUNK)
            ]
            scored, soft, totals = {}, {}, {}
            for u in range(-1, len(units) + 1):
                if u + 1 < len(units):
                    head, tok = units[u + 1]
                    if tok.start == 0 and head in starts:
                        await_rows(starts.index(head))
                    hc = slice(head * HD, (head + 1) * HD)
                    scored[u + 1] = score(
                        q_buf[tok, hc], kv_buf[0, :, hc], kv_buf[1, :, hc], g_buf[tok, hc]
                    )
                if 0 <= u - 1:
                    head, tok = units[u - 1]
                    hc = slice(head * HD, (head + 1) * HD)
                    ds, probs = soft.pop(u - 1)
                    gk, gv = dot_nn(ds, q_buf[tok, hc]), dot_nn(probs, g_buf[tok, hc])
                    if head in totals:
                        gk, gv = totals[head][0] + gk, totals[head][1] + gv
                    totals[head] = (gk, gv)
                    if tok.stop == tokens:
                        parts[0, :, hc] = (gk * SCALE).astype(BF16)
                        parts[1, :, hc] = gv.astype(BF16)
                if 0 <= u < len(units):
                    head, tok = units[u]
                    ds, probs = soften(*scored.pop(u))
                    ds_buf[head, :, tok] = ds
                    soft[u] = (ds, probs)
        else:
            for head in range(g * per, (g + 1) * per):
                if head in starts:
                    await_rows(starts.index(head))
            lax.fori_loop(g * per, (g + 1) * per, lambda h, c: (one_head(h), c)[1], 0)

        def send_parts(k, g=g, cols=cols):
            to = lax.rem(me + k, n)
            pltpu.make_async_remote_copy(
                src_ref=parts.at[:, pl.ds(pl.multiple_of(to * own, own), own), cols],
                dst_ref=got.at[:, pl.ds((k - 1) * own, own), cols],
                send_sem=aa_send,
                recv_sem=aa_recv.at[g],
                device_id={"seq": to},
                device_id_type=MESH,
            ).start()

        each(1, n, send_parts)

    def query_grads(g):
        def one_head(head):
            if isinstance(head, int):
                hc = pl.ds(head * HD, HD)
            else:
                hc = pl.ds(pl.multiple_of(head * HD, HD), HD)
            gq_buf[:, hc] = (dot_tn(ds_buf[head], kv_buf[0, :, hc]) * SCALE).astype(BF16)

        if small:
            for head in range(g * per, (g + 1) * per):
                one_head(head)
        else:
            lax.fori_loop(g * per, (g + 1) * per, lambda h, c: (one_head(h), c)[1], 0)

    for copy in w_copies:
        copy.wait()
    rs_copies = []
    for g in range(groups):
        if g == 0:
            query_grads(g)
        cols = pl.ds(g * gw, gw)
        arrived = got.at[:, :, cols]
        pltpu.make_async_copy(arrived, arrived, aa_recv.at[g]).wait()
        sides = []
        for side in range(2):
            total = parts[side, my_rows, cols].astype(F32)
            if n <= 8:
                for k in range(n - 1):
                    total += got[side, k * own : (k + 1) * own, cols].astype(F32)
            else:
                total = lax.fori_loop(
                    0,
                    n - 1,
                    lambda k, acc: acc
                    + got[side, pl.ds(pl.multiple_of(k * own, own), own), cols].astype(F32),
                    total,
                )
            high = total.astype(BF16)
            low = (total - high.astype(F32)).astype(BF16)
            sides.append(jnp.concatenate([high, low], axis=0))
        for j in range(1, nt + 1):
            to = lax.rem(mt + j, nt)
            wr = pl.ds(pl.multiple_of(to * out_cols, out_cols), out_cols)
            both = dot_nt(sides[0], w_buf[0, wr, cols]) + dot_nt(sides[1], w_buf[1, wr, cols])
            new = both[:own] + both[own:]
            if g:
                new = new + sums[j - 1]
            if g < groups - 1 or j == nt:
                sums[j - 1] = new
            else:
                out_send[j - 1] = new.astype(BF16)
                copy = pltpu.make_async_remote_copy(
                    src_ref=out_send.at[j - 1],
                    dst_ref=out_got.at[j - 1],
                    send_sem=rs_send.at[j - 1],
                    recv_sem=rs_recv.at[j - 1],
                    device_id={"tensor": to},
                    device_id_type=MESH,
                )
                copy.start()
                rs_copies.append(copy)

    for g in range(1, groups):
        query_grads(g)
    sent = kv_buf.at[:, others]
    pltpu.make_async_copy(sent, sent, ag_send).wait()
    pltpu.make_async_copy(got, got, aa_send).wait()
    total = sums[nt - 1]
    for j, copy in enumerate(rs_copies):
        copy.wait_recv()
        total += out_got[j].astype(F32)
    rows_ref[...] = total.astype(BF16)
    for copy in rs_copies:
        copy.wait_send()


def gather_cuts(heads):
    cuts = []
    at = 0
    while at < heads:
        count = min(1 if at < 2 else 2, heads - at)
        cuts.append((at, count))
        at += count
    return cuts


def deliver(gq_ref, rows_ref, gq_out, rows_out, sem):
    part = gq_ref.shape[0] // SPLIT
    copies = [pltpu.make_async_copy(rows_ref, rows_out, sem.at[SPLIT])]
    for i in range(SPLIT):
        rows = pl.ds(i * part, part)
        copies.append(pltpu.make_async_copy(gq_ref.at[rows], gq_out.at[rows], sem.at[i]))
    for copy in copies:
        copy.start()
    for copy in copies:
        copy.wait()


def solution(mesh):
    n, nt = mesh.shape["seq"], mesh.shape["tensor"]

    def shards(queries, ref_keys, ref_values, grad_out, key_weight, value_weight):
        tokens, width = queries.shape
        own = ref_keys.shape[0]
        features = key_weight.shape[0]
        heads = width // HD
        groups = 3 if heads % 3 == 0 else 1
        cuts = gather_cuts(heads)
        out_cols = features // nt
        hbm_spec = pl.BlockSpec(memory_space=pltpu.HBM)
        vmem_spec = pl.BlockSpec(memory_space=pltpu.VMEM)
        dma = pltpu.SemaphoreType.DMA
        held = pl.pallas_call(
            functools.partial(kernel, n, nt, groups, cuts),
            out_shape=(
                pltpu.VMEM((tokens, width), BF16),
                pltpu.VMEM((own, out_cols), BF16),
            ),
            in_specs=[hbm_spec] * 6,
            out_specs=(vmem_spec, vmem_spec),
            scratch_shapes=[
                pltpu.VMEM((tokens, width), BF16),
                pltpu.VMEM((tokens, width), BF16),
                pltpu.VMEM((heads, n * own, tokens), BF16),
                pltpu.VMEM((2, features, width), BF16),
                pltpu.VMEM((2, n * own, width), BF16),
                pltpu.VMEM((2, n * own, width), BF16),
                pltpu.VMEM((2, (n - 1) * own, width), BF16),
                pltpu.VMEM((nt, own, out_cols), F32),
                pltpu.VMEM((nt - 1, own, out_cols), BF16),
                pltpu.VMEM((nt - 1, own, out_cols), BF16),
                pltpu.VMEM((2, n * own, HD), F32),
                dma((2,)),
                dma((2,)),
                dma((2, nt)),
                dma,
                dma((len(cuts),)),
                dma,
                dma((groups,)),
                dma((nt - 1,)),
                dma((nt - 1,)),
            ],
            compiler_params=pltpu.CompilerParams(
                collective_id=0,
                has_side_effects=True,
                vmem_limit_bytes=VMEM_LIMIT,
            ),
            cost_estimate=pl.CostEstimate(
                flops=1_000_000_000, bytes_accessed=12_000_000, transcendentals=400_000
            ),
        )(
            *(
                pltpu.with_memory_space_constraint(x, pltpu.HBM)
                for x in (queries, ref_keys, ref_values, grad_out, key_weight, value_weight)
            )
        )
        return pl.pallas_call(
            deliver,
            out_shape=(
                jax.ShapeDtypeStruct((tokens, width), BF16),
                jax.ShapeDtypeStruct((own, out_cols), BF16),
            ),
            in_specs=[vmem_spec] * 2,
            out_specs=(hbm_spec, hbm_spec),
            scratch_shapes=[dma((SPLIT + 1,))],
        )(*(pltpu.with_memory_space_constraint(x, pltpu.VMEM) for x in held))

    placed = (
        P("seq", "tensor"),
        P("seq", "tensor"),
        P("seq", "tensor"),
        P("seq", "tensor"),
        P(None, "tensor"),
        P(None, "tensor"),
    )
    return jax.shard_map(
        shards,
        mesh=mesh,
        in_specs=placed,
        out_specs=(P("seq", "tensor"), P("seq", "tensor")),
        check_vma=False,
    )
```

```python
import functools
import math

import jax
import jax.numpy as jnp
from jax import lax
from jax.experimental import pallas as pl
from jax.experimental.pallas import tpu as pltpu
from jax.sharding import PartitionSpec as P

HD = 128
CHUNK = 256
SPLIT = 4
VMEM_LIMIT = 48 * 1024 * 1024
SCALE = 1.0 / HD**0.5
EXP_SCALE = SCALE * math.log2(math.e)
MESH = pl.DeviceIdType.MESH
F32 = jnp.float32
BF16 = jnp.bfloat16


def each(lo, hi, body):
    if hi - lo <= 8:
        for i in range(lo, hi):
            body(i)
    else:

        def step(i, carry):
            body(i)
            return carry

        lax.fori_loop(lo, hi, step, 0)


def dot_nt(a, b):
    return lax.dot_general(a, b, (((1,), (1,)), ((), ())), preferred_element_type=F32)


def dot_tn(a, b):
    return lax.dot_general(a, b, (((0,), (0,)), ((), ())), preferred_element_type=F32)


def dot_nn(a, b):
    return jnp.dot(a, b, preferred_element_type=F32)


def score(query, key, value, grad):
    return dot_nt(key, query), dot_nt(value, grad)


def soften(scores, grad_probs):
    top = jnp.max(scores, axis=0, keepdims=True)
    weights = jnp.exp2((scores - top) * EXP_SCALE)
    inverse = 1.0 / jnp.sum(weights, axis=0, keepdims=True)
    probs = weights * inverse
    delta = jnp.sum(probs * grad_probs, axis=0, keepdims=True)
    grad_scores = (probs * (grad_probs - delta)).astype(BF16)
    return grad_scores, probs.astype(BF16)


def attend(query, key, value, grad):
    grad_scores, probs = soften(*score(query, key, value, grad))
    return grad_scores, dot_nn(grad_scores, query), dot_nn(probs, grad)


def kernel(
    n,
    nt,
    groups,
    cuts,
    q_hbm,
    k_hbm,
    v_hbm,
    g_hbm,
    kw_hbm,
    vw_hbm,
    gq_buf,
    rows_ref,
    q_buf,
    g_buf,
    ds_buf,
    w_buf,
    kv_buf,
    parts,
    got,
    sums,
    out_send,
    out_got,
    head_acc,
    in_sem,
    own_sem,
    w_sem,
    ag_send,
    ag_recv,
    aa_send,
    aa_recv,
    rs_send,
    rs_recv,
):
    me = lax.axis_index("seq")
    mt = lax.axis_index("tensor")
    tokens, width = q_hbm.shape
    own = k_hbm.shape[0]
    heads = width // HD
    per = heads // groups
    gw = per * HD
    out_cols = rows_ref.shape[1]
    my_rows = pl.ds(pl.multiple_of(me * own, own), own)

    barrier = pltpu.get_barrier_semaphore()

    def greet_seq(k):
        pl.semaphore_signal(
            barrier, inc=1, device_id={"seq": lax.rem(me + k, n)}, device_id_type=MESH
        )

    def greet_tensor(k):
        pl.semaphore_signal(
            barrier, inc=1, device_id={"tensor": lax.rem(mt + k, nt)}, device_id_type=MESH
        )

    each(1, n, greet_seq)
    each(1, nt, greet_tensor)
    own_copies = [
        pltpu.make_async_copy(k_hbm, kv_buf.at[0, my_rows], own_sem.at[0]),
        pltpu.make_async_copy(v_hbm, kv_buf.at[1, my_rows], own_sem.at[1]),
    ]
    for copy in own_copies:
        copy.start()
    in_copies = [
        pltpu.make_async_copy(q_hbm, q_buf, in_sem.at[0]),
        pltpu.make_async_copy(g_hbm, g_buf, in_sem.at[1]),
    ]
    for copy in in_copies:
        copy.start()

    w_copies = []
    for b in range(nt):
        wr = pl.ds(b * out_cols, out_cols)
        for side, ref in enumerate((kw_hbm, vw_hbm)):
            w_copies.append(
                pltpu.make_async_copy(ref.at[wr], w_buf.at[side, wr], w_sem.at[side, b])
            )
    for copy in w_copies:
        copy.start()
    for copy in own_copies:
        copy.wait()
    pl.semaphore_wait(barrier, n + nt - 2)

    for c, (first, count) in enumerate(cuts):
        cols = pl.ds(first * HD, count * HD)

        def send_rows(k, c=c, cols=cols):
            block = kv_buf.at[:, my_rows, cols]
            pltpu.make_async_remote_copy(
                src_ref=block,
                dst_ref=block,
                send_sem=ag_send,
                recv_sem=ag_recv.at[c],
                device_id={"seq": lax.rem(me + k, n)},
                device_id_type=MESH,
            ).start()

        each(1, n, send_rows)

    for copy in in_copies:
        copy.wait()

    ref_rows = n * own
    others = pl.ds(0, (n - 1) * own)
    small = ref_rows <= 256

    def await_rows(c):
        first, count = cuts[c]
        arrived = kv_buf.at[:, others, pl.ds(first * HD, count * HD)]
        pltpu.make_async_copy(arrived, arrived, ag_recv.at[c]).wait()

    starts = [first for first, _ in cuts]
    for g in range(groups):
        cols = pl.ds(g * gw, gw)

        def one_head(head):
            if isinstance(head, int):
                hc = pl.ds(head * HD, HD)
            else:
                hc = pl.ds(pl.multiple_of(head * HD, HD), HD)
            key = kv_buf[0, :, hc]
            value = kv_buf[1, :, hc]
            head_acc[...] = jnp.zeros_like(head_acc)

            def chunk(c, carry):
                tok = pl.ds(pl.multiple_of(c * HD, HD), HD)
                ds, gk, gv = attend(q_buf[tok, hc], key, value, g_buf[tok, hc])
                ds_buf[head, :, tok] = ds
                head_acc[0] += gk
                head_acc[1] += gv
                return carry

            lax.fori_loop(0, tokens // HD, chunk, 0)
            grad_key, grad_value = head_acc[0], head_acc[1]
            parts[0, :, hc] = (grad_key * SCALE).astype(BF16)
            parts[1, :, hc] = grad_value.astype(BF16)

        if small:
            units = [
                (head, slice(lo, min(lo + CHUNK, tokens)))
                for head in range(g * per, (g + 1) * per)
                for lo in range(0, tokens, CHUNK)
            ]
            scored, soft, totals = {}, {}, {}
            for u in range(-1, len(units) + 1):
                if u + 1 < len(units):
                    head, tok = units[u + 1]
                    if tok.start == 0 and head in starts:
                        await_rows(starts.index(head))
                    hc = slice(head * HD, (head + 1) * HD)
                    scored[u + 1] = score(
                        q_buf[tok, hc], kv_buf[0, :, hc], kv_buf[1, :, hc], g_buf[tok, hc]
                    )
                if 0 <= u - 1:
                    head, tok = units[u - 1]
                    hc = slice(head * HD, (head + 1) * HD)
                    ds, probs = soft.pop(u - 1)
                    gk, gv = dot_nn(ds, q_buf[tok, hc]), dot_nn(probs, g_buf[tok, hc])
                    if head in totals:
                        gk, gv = totals[head][0] + gk, totals[head][1] + gv
                    totals[head] = (gk, gv)
                    if tok.stop == tokens:
                        parts[0, :, hc] = (gk * SCALE).astype(BF16)
                        parts[1, :, hc] = gv.astype(BF16)
                if 0 <= u < len(units):
                    head, tok = units[u]
                    ds, probs = soften(*scored.pop(u))
                    ds_buf[head, :, tok] = ds
                    soft[u] = (ds, probs)
        else:
            for head in range(g * per, (g + 1) * per):
                if head in starts:
                    await_rows(starts.index(head))
            lax.fori_loop(g * per, (g + 1) * per, lambda h, c: (one_head(h), c)[1], 0)

        def send_parts(k, g=g, cols=cols):
            to = lax.rem(me + k, n)
            pltpu.make_async_remote_copy(
                src_ref=parts.at[:, pl.ds(pl.multiple_of(to * own, own), own), cols],
                dst_ref=got.at[:, pl.ds((k - 1) * own, own), cols],
                send_sem=aa_send,
                recv_sem=aa_recv.at[g],
                device_id={"seq": to},
                device_id_type=MESH,
            ).start()

        each(1, n, send_parts)

    def query_grads(g):
        def one_head(head):
            if isinstance(head, int):
                hc = pl.ds(head * HD, HD)
            else:
                hc = pl.ds(pl.multiple_of(head * HD, HD), HD)
            gq_buf[:, hc] = (dot_tn(ds_buf[head], kv_buf[0, :, hc]) * SCALE).astype(BF16)

        if small:
            for head in range(g * per, (g + 1) * per):
                one_head(head)
        else:
            lax.fori_loop(g * per, (g + 1) * per, lambda h, c: (one_head(h), c)[1], 0)

    for copy in w_copies:
        copy.wait()
    rs_copies = []
    for g in range(groups):
        if g < groups - 1:
            query_grads(g)
        cols = pl.ds(g * gw, gw)
        arrived = got.at[:, :, cols]
        pltpu.make_async_copy(arrived, arrived, aa_recv.at[g]).wait()
        sides = []
        for side in range(2):
            total = parts[side, my_rows, cols].astype(F32)
            if n <= 8:
                for k in range(n - 1):
                    total += got[side, k * own : (k + 1) * own, cols].astype(F32)
            else:
                total = lax.fori_loop(
                    0,
                    n - 1,
                    lambda k, acc: acc
                    + got[side, pl.ds(pl.multiple_of(k * own, own), own), cols].astype(F32),
                    total,
                )
            high = total.astype(BF16)
            low = (total - high.astype(F32)).astype(BF16)
            sides.append(jnp.concatenate([high, low], axis=0))
        for j in range(1, nt + 1):
            to = lax.rem(mt + j, nt)
            wr = pl.ds(pl.multiple_of(to * out_cols, out_cols), out_cols)
            both = dot_nt(sides[0], w_buf[0, wr, cols]) + dot_nt(sides[1], w_buf[1, wr, cols])
            new = both[:own] + both[own:]
            if g:
                new = new + sums[j - 1]
            if g < groups - 1 or j == nt:
                sums[j - 1] = new
            else:
                out_send[j - 1] = new.astype(BF16)
                copy = pltpu.make_async_remote_copy(
                    src_ref=out_send.at[j - 1],
                    dst_ref=out_got.at[j - 1],
                    send_sem=rs_send.at[j - 1],
                    recv_sem=rs_recv.at[j - 1],
                    device_id={"tensor": to},
                    device_id_type=MESH,
                )
                copy.start()
                rs_copies.append(copy)

    query_grads(groups - 1)
    sent = kv_buf.at[:, others]
    pltpu.make_async_copy(sent, sent, ag_send).wait()
    pltpu.make_async_copy(got, got, aa_send).wait()
    total = sums[nt - 1]
    for j, copy in enumerate(rs_copies):
        copy.wait_recv()
        total += out_got[j].astype(F32)
    rows_ref[...] = total.astype(BF16)
    for copy in rs_copies:
        copy.wait_send()


def gather_cuts(heads):
    cuts = []
    at = 0
    while at < heads:
        count = min(2, heads - at)
        cuts.append((at, count))
        at += count
    return cuts


def deliver(gq_ref, rows_ref, gq_out, rows_out, sem):
    part = gq_ref.shape[0] // SPLIT
    copies = [pltpu.make_async_copy(rows_ref, rows_out, sem.at[SPLIT])]
    for i in range(SPLIT):
        rows = pl.ds(i * part, part)
        copies.append(pltpu.make_async_copy(gq_ref.at[rows], gq_out.at[rows], sem.at[i]))
    for copy in copies:
        copy.start()
    for copy in copies:
        copy.wait()


def solution(mesh):
    n, nt = mesh.shape["seq"], mesh.shape["tensor"]

    def shards(queries, ref_keys, ref_values, grad_out, key_weight, value_weight):
        tokens, width = queries.shape
        own = ref_keys.shape[0]
        features = key_weight.shape[0]
        heads = width // HD
        groups = 3 if heads % 3 == 0 else 1
        cuts = gather_cuts(heads)
        out_cols = features // nt
        hbm_spec = pl.BlockSpec(memory_space=pltpu.HBM)
        vmem_spec = pl.BlockSpec(memory_space=pltpu.VMEM)
        dma = pltpu.SemaphoreType.DMA
        held = pl.pallas_call(
            functools.partial(kernel, n, nt, groups, cuts),
            out_shape=(
                pltpu.VMEM((tokens, width), BF16),
                pltpu.VMEM((own, out_cols), BF16),
            ),
            in_specs=[hbm_spec] * 6,
            out_specs=(vmem_spec, vmem_spec),
            scratch_shapes=[
                pltpu.VMEM((tokens, width), BF16),
                pltpu.VMEM((tokens, width), BF16),
                pltpu.VMEM((heads, n * own, tokens), BF16),
                pltpu.VMEM((2, features, width), BF16),
                pltpu.VMEM((2, n * own, width), BF16),
                pltpu.VMEM((2, n * own, width), BF16),
                pltpu.VMEM((2, (n - 1) * own, width), BF16),
                pltpu.VMEM((nt, own, out_cols), F32),
                pltpu.VMEM((nt - 1, own, out_cols), BF16),
                pltpu.VMEM((nt - 1, own, out_cols), BF16),
                pltpu.VMEM((2, n * own, HD), F32),
                dma((2,)),
                dma((2,)),
                dma((2, nt)),
                dma,
                dma((len(cuts),)),
                dma,
                dma((groups,)),
                dma((nt - 1,)),
                dma((nt - 1,)),
            ],
            compiler_params=pltpu.CompilerParams(
                collective_id=0,
                has_side_effects=True,
                vmem_limit_bytes=VMEM_LIMIT,
            ),
            cost_estimate=pl.CostEstimate(
                flops=1_000_000_000, bytes_accessed=12_000_000, transcendentals=400_000
            ),
        )(
            *(
                pltpu.with_memory_space_constraint(x, pltpu.HBM)
                for x in (queries, ref_keys, ref_values, grad_out, key_weight, value_weight)
            )
        )
        return pl.pallas_call(
            deliver,
            out_shape=(
                jax.ShapeDtypeStruct((tokens, width), BF16),
                jax.ShapeDtypeStruct((own, out_cols), BF16),
            ),
            in_specs=[vmem_spec] * 2,
            out_specs=(hbm_spec, hbm_spec),
            scratch_shapes=[dma((SPLIT + 1,))],
        )(*(pltpu.with_memory_space_constraint(x, pltpu.VMEM) for x in held))

    placed = (
        P("seq", "tensor"),
        P("seq", "tensor"),
        P("seq", "tensor"),
        P("seq", "tensor"),
        P(None, "tensor"),
        P(None, "tensor"),
    )
    return jax.shard_map(
        shards,
        mesh=mesh,
        in_specs=placed,
        out_specs=(P("seq", "tensor"), P("seq", "tensor")),
        check_vma=False,
    )
```

```python
import functools
import math

import jax
import jax.numpy as jnp
from jax import lax
from jax.experimental import pallas as pl
from jax.experimental.pallas import tpu as pltpu
from jax.sharding import PartitionSpec as P

HD = 128
CHUNK = 256
SPLIT = 4
VMEM_LIMIT = 48 * 1024 * 1024
SCALE = 1.0 / HD**0.5
EXP_SCALE = SCALE * math.log2(math.e)
MESH = pl.DeviceIdType.MESH
F32 = jnp.float32
BF16 = jnp.bfloat16


def each(lo, hi, body):
    if hi - lo <= 8:
        for i in range(lo, hi):
            body(i)
    else:

        def step(i, carry):
            body(i)
            return carry

        lax.fori_loop(lo, hi, step, 0)


def dot_nt(a, b):
    return lax.dot_general(a, b, (((1,), (1,)), ((), ())), preferred_element_type=F32)


def dot_tn(a, b):
    return lax.dot_general(a, b, (((0,), (0,)), ((), ())), preferred_element_type=F32)


def dot_nn(a, b):
    return jnp.dot(a, b, preferred_element_type=F32)


def score(query, key, value, grad):
    return dot_nt(key, query), dot_nt(value, grad)


def soften(scores, grad_probs):
    top = jnp.max(scores, axis=0, keepdims=True)
    weights = jnp.exp2((scores - top) * EXP_SCALE)
    inverse = 1.0 / jnp.sum(weights, axis=0, keepdims=True)
    probs = weights * inverse
    delta = jnp.sum(probs * grad_probs, axis=0, keepdims=True)
    grad_scores = (probs * (grad_probs - delta)).astype(BF16)
    return grad_scores, probs.astype(BF16)


def attend(query, key, value, grad):
    grad_scores, probs = soften(*score(query, key, value, grad))
    return grad_scores, dot_nn(grad_scores, query), dot_nn(probs, grad)


def kernel(
    n,
    nt,
    groups,
    cuts,
    q_hbm,
    k_hbm,
    v_hbm,
    g_hbm,
    kw_hbm,
    vw_hbm,
    gq_buf,
    rows_ref,
    q_buf,
    g_buf,
    ds_buf,
    w_buf,
    kv_buf,
    parts,
    got,
    sums,
    out_send,
    out_got,
    head_acc,
    in_sem,
    own_sem,
    w_sem,
    ag_send,
    ag_recv,
    aa_send,
    aa_recv,
    rs_send,
    rs_recv,
):
    me = lax.axis_index("seq")
    mt = lax.axis_index("tensor")
    tokens, width = q_hbm.shape
    own = k_hbm.shape[0]
    heads = width // HD
    per = heads // groups
    gw = per * HD
    out_cols = rows_ref.shape[1]
    my_rows = pl.ds(pl.multiple_of(me * own, own), own)

    barrier = pltpu.get_barrier_semaphore()

    def greet_seq(k):
        pl.semaphore_signal(
            barrier, inc=1, device_id={"seq": lax.rem(me + k, n)}, device_id_type=MESH
        )

    def greet_tensor(k):
        pl.semaphore_signal(
            barrier, inc=1, device_id={"tensor": lax.rem(mt + k, nt)}, device_id_type=MESH
        )

    each(1, n, greet_seq)
    each(1, nt, greet_tensor)
    own_copies = [
        pltpu.make_async_copy(k_hbm, kv_buf.at[0, my_rows], own_sem.at[0]),
        pltpu.make_async_copy(v_hbm, kv_buf.at[1, my_rows], own_sem.at[1]),
    ]
    for copy in own_copies:
        copy.start()
    in_copies = [
        pltpu.make_async_copy(q_hbm, q_buf, in_sem.at[0]),
        pltpu.make_async_copy(g_hbm, g_buf, in_sem.at[1]),
    ]
    for copy in in_copies:
        copy.start()

    for copy in own_copies:
        copy.wait()
    pl.semaphore_wait(barrier, n + nt - 2)

    for c, (first, count) in enumerate(cuts):
        cols = pl.ds(first * HD, count * HD)

        def send_rows(k, c=c, cols=cols):
            block = kv_buf.at[:, my_rows, cols]
            pltpu.make_async_remote_copy(
                src_ref=block,
                dst_ref=block,
                send_sem=ag_send,
                recv_sem=ag_recv.at[c],
                device_id={"seq": lax.rem(me + k, n)},
                device_id_type=MESH,
            ).start()

        each(1, n, send_rows)

    w_copies = []
    for b in range(nt):
        wr = pl.ds(b * out_cols, out_cols)
        for side, ref in enumerate((kw_hbm, vw_hbm)):
            w_copies.append(
                pltpu.make_async_copy(ref.at[wr], w_buf.at[side, wr], w_sem.at[side, b])
            )
    lot = -(-len(w_copies) // groups)
    for copy in w_copies[:lot]:
        copy.start()
    for copy in in_copies:
        copy.wait()

    ref_rows = n * own
    others = pl.ds(0, (n - 1) * own)
    small = ref_rows <= 256

    def await_rows(c):
        first, count = cuts[c]
        arrived = kv_buf.at[:, others, pl.ds(first * HD, count * HD)]
        pltpu.make_async_copy(arrived, arrived, ag_recv.at[c]).wait()

    starts = [first for first, _ in cuts]
    for g in range(groups):
        cols = pl.ds(g * gw, gw)

        def one_head(head):
            if isinstance(head, int):
                hc = pl.ds(head * HD, HD)
            else:
                hc = pl.ds(pl.multiple_of(head * HD, HD), HD)
            key = kv_buf[0, :, hc]
            value = kv_buf[1, :, hc]
            head_acc[...] = jnp.zeros_like(head_acc)

            def chunk(c, carry):
                tok = pl.ds(pl.multiple_of(c * HD, HD), HD)
                ds, gk, gv = attend(q_buf[tok, hc], key, value, g_buf[tok, hc])
                ds_buf[head, :, tok] = ds
                head_acc[0] += gk
                head_acc[1] += gv
                return carry

            lax.fori_loop(0, tokens // HD, chunk, 0)
            grad_key, grad_value = head_acc[0], head_acc[1]
            parts[0, :, hc] = (grad_key * SCALE).astype(BF16)
            parts[1, :, hc] = grad_value.astype(BF16)

        if small:
            units = [
                (head, slice(lo, min(lo + CHUNK, tokens)))
                for head in range(g * per, (g + 1) * per)
                for lo in range(0, tokens, CHUNK)
            ]
            scored, soft, totals = {}, {}, {}
            for u in range(-1, len(units) + 1):
                if u + 1 < len(units):
                    head, tok = units[u + 1]
                    if tok.start == 0 and head in starts:
                        await_rows(starts.index(head))
                    hc = slice(head * HD, (head + 1) * HD)
                    scored[u + 1] = score(
                        q_buf[tok, hc], kv_buf[0, :, hc], kv_buf[1, :, hc], g_buf[tok, hc]
                    )
                if 0 <= u - 1:
                    head, tok = units[u - 1]
                    hc = slice(head * HD, (head + 1) * HD)
                    ds, probs = soft.pop(u - 1)
                    gk, gv = dot_nn(ds, q_buf[tok, hc]), dot_nn(probs, g_buf[tok, hc])
                    if head in totals:
                        gk, gv = totals[head][0] + gk, totals[head][1] + gv
                    totals[head] = (gk, gv)
                    if tok.stop == tokens:
                        parts[0, :, hc] = (gk * SCALE).astype(BF16)
                        parts[1, :, hc] = gv.astype(BF16)
                if 0 <= u < len(units):
                    head, tok = units[u]
                    ds, probs = soften(*scored.pop(u))
                    ds_buf[head, :, tok] = ds
                    soft[u] = (ds, probs)
        else:
            for head in range(g * per, (g + 1) * per):
                if head in starts:
                    await_rows(starts.index(head))
            lax.fori_loop(g * per, (g + 1) * per, lambda h, c: (one_head(h), c)[1], 0)

        def send_parts(k, g=g, cols=cols):
            to = lax.rem(me + k, n)
            pltpu.make_async_remote_copy(
                src_ref=parts.at[:, pl.ds(pl.multiple_of(to * own, own), own), cols],
                dst_ref=got.at[:, pl.ds((k - 1) * own, own), cols],
                send_sem=aa_send,
                recv_sem=aa_recv.at[g],
                device_id={"seq": to},
                device_id_type=MESH,
            ).start()

        each(1, n, send_parts)
        for copy in w_copies[(g + 1) * lot : (g + 2) * lot]:
            copy.start()

    def query_grads(g):
        def one_head(head):
            if isinstance(head, int):
                hc = pl.ds(head * HD, HD)
            else:
                hc = pl.ds(pl.multiple_of(head * HD, HD), HD)
            gq_buf[:, hc] = (dot_tn(ds_buf[head], kv_buf[0, :, hc]) * SCALE).astype(BF16)

        if small:
            for head in range(g * per, (g + 1) * per):
                one_head(head)
        else:
            lax.fori_loop(g * per, (g + 1) * per, lambda h, c: (one_head(h), c)[1], 0)

    for copy in w_copies:
        copy.wait()
    rs_copies = []
    for g in range(groups):
        if g == 0:
            query_grads(g)
        cols = pl.ds(g * gw, gw)
        arrived = got.at[:, :, cols]
        pltpu.make_async_copy(arrived, arrived, aa_recv.at[g]).wait()
        sides = []
        for side in range(2):
            total = parts[side, my_rows, cols].astype(F32)
            if n <= 8:
                for k in range(n - 1):
                    total += got[side, k * own : (k + 1) * own, cols].astype(F32)
            else:
                total = lax.fori_loop(
                    0,
                    n - 1,
                    lambda k, acc: acc
                    + got[side, pl.ds(pl.multiple_of(k * own, own), own), cols].astype(F32),
                    total,
                )
            high = total.astype(BF16)
            low = (total - high.astype(F32)).astype(BF16)
            sides.append(jnp.concatenate([high, low], axis=0))
        for j in range(1, nt + 1):
            to = lax.rem(mt + j, nt)
            wr = pl.ds(pl.multiple_of(to * out_cols, out_cols), out_cols)
            both = dot_nt(sides[0], w_buf[0, wr, cols]) + dot_nt(sides[1], w_buf[1, wr, cols])
            new = both[:own] + both[own:]
            if g:
                new = new + sums[j - 1]
            if g < groups - 1 or j == nt:
                sums[j - 1] = new
            else:
                out_send[j - 1] = new.astype(BF16)
                copy = pltpu.make_async_remote_copy(
                    src_ref=out_send.at[j - 1],
                    dst_ref=out_got.at[j - 1],
                    send_sem=rs_send.at[j - 1],
                    recv_sem=rs_recv.at[j - 1],
                    device_id={"tensor": to},
                    device_id_type=MESH,
                )
                copy.start()
                rs_copies.append(copy)

    for g in range(1, groups):
        query_grads(g)
    sent = kv_buf.at[:, others]
    pltpu.make_async_copy(sent, sent, ag_send).wait()
    pltpu.make_async_copy(got, got, aa_send).wait()
    total = sums[nt - 1]
    for j, copy in enumerate(rs_copies):
        copy.wait_recv()
        total += out_got[j].astype(F32)
    rows_ref[...] = total.astype(BF16)
    for copy in rs_copies:
        copy.wait_send()


def gather_cuts(heads):
    cuts = []
    at = 0
    while at < heads:
        count = min(1 if at < 2 else 2, heads - at)
        cuts.append((at, count))
        at += count
    return cuts


def deliver(gq_ref, rows_ref, gq_out, rows_out, sem):
    part = gq_ref.shape[0] // SPLIT
    copies = [pltpu.make_async_copy(rows_ref, rows_out, sem.at[SPLIT])]
    for i in range(SPLIT):
        rows = pl.ds(i * part, part)
        copies.append(pltpu.make_async_copy(gq_ref.at[rows], gq_out.at[rows], sem.at[i]))
    for copy in copies:
        copy.start()
    for copy in copies:
        copy.wait()


def solution(mesh):
    n, nt = mesh.shape["seq"], mesh.shape["tensor"]

    def shards(queries, ref_keys, ref_values, grad_out, key_weight, value_weight):
        tokens, width = queries.shape
        own = ref_keys.shape[0]
        features = key_weight.shape[0]
        heads = width // HD
        groups = 3 if heads % 3 == 0 else 1
        cuts = gather_cuts(heads)
        out_cols = features // nt
        hbm_spec = pl.BlockSpec(memory_space=pltpu.HBM)
        vmem_spec = pl.BlockSpec(memory_space=pltpu.VMEM)
        dma = pltpu.SemaphoreType.DMA
        held = pl.pallas_call(
            functools.partial(kernel, n, nt, groups, cuts),
            out_shape=(
                pltpu.VMEM((tokens, width), BF16),
                pltpu.VMEM((own, out_cols), BF16),
            ),
            in_specs=[hbm_spec] * 6,
            out_specs=(vmem_spec, vmem_spec),
            scratch_shapes=[
                pltpu.VMEM((tokens, width), BF16),
                pltpu.VMEM((tokens, width), BF16),
                pltpu.VMEM((heads, n * own, tokens), BF16),
                pltpu.VMEM((2, features, width), BF16),
                pltpu.VMEM((2, n * own, width), BF16),
                pltpu.VMEM((2, n * own, width), BF16),
                pltpu.VMEM((2, (n - 1) * own, width), BF16),
                pltpu.VMEM((nt, own, out_cols), F32),
                pltpu.VMEM((nt - 1, own, out_cols), BF16),
                pltpu.VMEM((nt - 1, own, out_cols), BF16),
                pltpu.VMEM((2, n * own, HD), F32),
                dma((2,)),
                dma((2,)),
                dma((2, nt)),
                dma,
                dma((len(cuts),)),
                dma,
                dma((groups,)),
                dma((nt - 1,)),
                dma((nt - 1,)),
            ],
            compiler_params=pltpu.CompilerParams(
                collective_id=0,
                has_side_effects=True,
                vmem_limit_bytes=VMEM_LIMIT,
            ),
            cost_estimate=pl.CostEstimate(
                flops=1_000_000_000, bytes_accessed=12_000_000, transcendentals=400_000
            ),
        )(
            *(
                pltpu.with_memory_space_constraint(x, pltpu.HBM)
                for x in (queries, ref_keys, ref_values, grad_out, key_weight, value_weight)
            )
        )
        return pl.pallas_call(
            deliver,
            out_shape=(
                jax.ShapeDtypeStruct((tokens, width), BF16),
                jax.ShapeDtypeStruct((own, out_cols), BF16),
            ),
            in_specs=[vmem_spec] * 2,
            out_specs=(hbm_spec, hbm_spec),
            scratch_shapes=[dma((SPLIT + 1,))],
        )(*(pltpu.with_memory_space_constraint(x, pltpu.VMEM) for x in held))

    placed = (
        P("seq", "tensor"),
        P("seq", "tensor"),
        P("seq", "tensor"),
        P("seq", "tensor"),
        P(None, "tensor"),
        P(None, "tensor"),
    )
    return jax.shard_map(
        shards,
        mesh=mesh,
        in_specs=placed,
        out_specs=(P("seq", "tensor"), P("seq", "tensor")),
        check_vma=False,
    )
```
